256 devices in a mesh: blk: 32 (over y_hi, z, core), phase: 8 (over y_lo, x).
Axes of the slice: x: 4, y: 4 (y_hi: 2, y_lo: 2; y = y_hi * 2 + y_lo), z: 8, core: 2. Of those that a mesh axis runs over, the one named last changes fastest.
Arguments:
- acts: bfloat16 [8, 4096, 2048], P('phase', 'blk'), may hold values from -6 to 6
- order: int32 [4096], replicated, may hold values from 0 to 4095, each once
- doc_ids: int32 [4096], replicated, may hold values from 0 to 7, never falling along the last dimension, each value on 1 to 1024 neighbouring positions
- gain: float32 [8, 2048], P('phase'), may hold values from 0.1 to 1.9
- w_query: bfloat16 [8, 2048, 1024], P('phase'), may hold values from -0.125 to 0.125
- w_keyval: bfloat16 [8, 2048, 2048], P('phase', 'blk'), may hold values from -0.125 to 0.125
- w_out: bfloat16 [8, 1024, 2048], P('phase'), may hold values from -0.5 to 0.5
- head_temp: float32 [8, 8], P('phase'), may hold values from 1 to 400
Outputs:
- layer_out: bfloat16 [8, 4096, 2048], P('phase', 'blk')
- next_input: bfloat16 [8, 4096, 2048], P('phase', 'blk')
The draws below stay inside these ranges and needn't reach their ends.
Inputs may be any that keep to these rules, and one draw needn't show every extreme that they name: order holds every position of the sequence once. doc_ids never falls along positions; each document covers 1 to 1024 positions and one covers exactly 1024.
All inputs are finite; a program needn't handle non-finite values.
Results may differ from the reference program's by a relative error of at most 0.006.
The reference program's roundings to bfloat16 on the way count: a program that leaves them out, or rounds other values in their place, can miss the bound.
Values may be sent and summed in bfloat16 or wider, within the bound.
No kernel may reach another device: no remote copies, remote signals or barrier semaphores. Data moves between devices by JAX's collectives and lax.ppermute only.
A program may use at most 128 MiB of HBM per device.

```python
import math
import jax
import jax.numpy as jnp
import numpy as np
from jax import lax

D = 2048
HEADS = 8
HDIM = 128
DOCS = 8
TOKENS = 4096
LAYERS = 8


def draw_head_temp(key, part):
    uniform_draw = jax.random.uniform(key, (LAYERS, HEADS), jnp.float32)
    low = math.log(2.0)
    high = math.log(24.0)
    return jnp.exp(low + uniform_draw * (high - low)).astype(jnp.float32)


def shard_levels(own_key, dims, cuts, low, high):
    level, own = 1.0, jax.random.fold_in(own_key, 6)
    for position, parts in cuts:
        draws = jnp.exp(jax.random.uniform(jax.random.fold_in(own, position), (parts,), jnp.float32, low / len(cuts), high / len(cuts)))
        level = level * jnp.repeat(draws, dims[position] // parts).reshape([-1 if axis == position else 1 for axis in range(len(dims))])
    return level


def length_profile(number_of, total, most, skew):
    portions = [(1 << 20) // math.isqrt(rank ** skew) + 1 for rank in range(2, number_of + 1)]
    surplus, given = total - most - (number_of - 1), [1] * (number_of - 1)
    while surplus > 0:
        movable = [i for i in range(number_of - 1) if given[i] < most]
        mass, budget = sum([portions[i] for i in movable]), surplus
        for i in movable:
            extra = min(most - given[i], max(1, budget * portions[i] // mass), surplus)
            given[i] = given[i] + extra
            surplus = surplus - extra
    return np.array([most] + given)


def ragged_sizes(own_key, amount, total, reach, skew):
    if amount == 2:
        one = jax.random.randint(own_key, (), max(1, total - reach), min(reach, total - 1) + 1)
        return jnp.stack([one, total - one])
    tallies = jnp.asarray(length_profile(amount, total, reach, skew), jnp.int32)
    couples = (amount - 1) // 2
    giver, taker = tallies[1:1 + 2 * couples:2], tallies[2:2 + 2 * couples:2]
    room = jnp.minimum(giver - 1, reach - taker)
    passed = jax.random.randint(jax.random.fold_in(own_key, 1), (couples,), 0, 1 << 20) % (room + 1)
    tallies = tallies.at[1:1 + 2 * couples:2].set(giver - passed).at[2:2 + 2 * couples:2].set(taker + passed)
    return tallies[jax.random.permutation(jax.random.fold_in(own_key, 2), amount)]


def bell_draw(rng, extent, scale, most, split=(), held_as=jnp.bfloat16):
    values = scale * jax.random.normal(rng, extent, jnp.float32)
    if split:
        values = values * shard_levels(rng, extent, split, -0.22, 0.18)
    return jnp.clip(values, -most, most).astype(held_as)


def setup_inputs(seed: int = 0) -> dict:
    splits = jax.random.split(jax.random.key(seed), 9)
    return {
        "acts": bell_draw(splits[0], (LAYERS, TOKENS, D), 1.0, 6.0, ((0, 8), (1, 32))),
        "order": jax.random.permutation(splits[1], TOKENS).astype(jnp.int32),
        "doc_ids": jnp.searchsorted(jnp.cumsum(ragged_sizes(splits[2], DOCS, TOKENS, TOKENS // 4, 0)), jnp.arange(TOKENS), side="right").astype(jnp.int32),
        "gain": jnp.clip(1.0 + 0.18 * jax.random.normal(splits[3], (LAYERS, D), jnp.float32), 0.1, 1.9),
        "w_query": bell_draw(splits[4], (LAYERS, D, HEADS * HDIM), D ** -0.5, 0.125, ((0, 8),)),
        "w_keyval": bell_draw(splits[5], (LAYERS, D, 2 * HEADS * HDIM), D ** -0.5, 0.125, ((0, 8), (1, 32))),
        "w_out": bell_draw(splits[6], (LAYERS, HEADS * HDIM, D), (3.0 / (HEADS * HDIM) ** 0.5), 0.5, ((0, 8),)),
        "head_temp": draw_head_temp(jax.random.fold_in(splits[8], 71), 0),
    }


def reference(acts, order, doc_ids, gain, w_query, w_keyval, w_out, head_temp):
    documents = jnp.take(doc_ids, order)
    visible = (order[None, :] <= order[:, None]) & (documents[None, :] == documents[:, None])
    attn_width = HEADS * HDIM
    results = []
    for layer_index in range(LAYERS):
        upcast = acts[layer_index].astype(jnp.float32)
        normed = (upcast * lax.rsqrt(lax.optimization_barrier(jnp.mean(upcast * upcast, axis=-1, keepdims=True)) + 1e-05) * gain[layer_index].astype(jnp.float32)).astype(jnp.bfloat16)
        queries = jnp.dot(normed, w_query[layer_index], preferred_element_type=jnp.float32)
        queries = queries.reshape(TOKENS, HEADS, HDIM)
        keyval = jnp.dot(normed, w_keyval[layer_index], preferred_element_type=jnp.float32)
        keys = keyval[:, :attn_width].reshape(TOKENS, HEADS, HDIM)
        values = keyval[:, attn_width:].astype(jnp.bfloat16)
        temps = head_temp[layer_index].astype(jnp.float32)[None, :, None]
        q_norm = (queries * lax.rsqrt(lax.optimization_barrier(jnp.mean(queries * queries, axis=-1, keepdims=True)) + 1e-06) * temps / HDIM).astype(jnp.bfloat16)
        k_norm = (keys * lax.rsqrt(lax.optimization_barrier(jnp.mean(keys * keys, axis=-1, keepdims=True)) + 1e-06)).astype(jnp.bfloat16)
        pieces = []
        for head_index in range(HEADS):
            scores = jnp.dot(q_norm[:, head_index, :], k_norm[:, head_index, :].T, preferred_element_type=jnp.float32)
            masked = jnp.where(visible, scores, -jnp.inf)
            peak = lax.optimization_barrier(jnp.max(masked, axis=-1, keepdims=True))
            weights = jnp.where(visible, jnp.exp(masked - peak), jnp.zeros_like(scores))
            head_values = values[:, head_index * HDIM:(head_index + 1) * HDIM].astype(jnp.float32)
            summed = jnp.dot(weights, head_values, precision=lax.Precision.HIGHEST, preferred_element_type=jnp.float32)
            pieces.append(summed / lax.optimization_barrier(jnp.sum(weights, axis=-1, keepdims=True)))
        mixed = jnp.concatenate(pieces, axis=1).astype(jnp.bfloat16)
        results.append((upcast + jnp.dot(mixed, w_out[layer_index], preferred_element_type=jnp.float32)).astype(jnp.bfloat16))
    layer_out = jnp.stack(results)
    next_input = jnp.concatenate([jnp.zeros_like(layer_out[:1]), layer_out[:-1]], axis=0)
    return (layer_out, next_input)
```

```python
import functools

import jax
import jax.numpy as jnp
import numpy as np
from jax import lax
from jax.experimental import pallas as pl
from jax.experimental.pallas import tpu as pltpu
from jax.sharding import Mesh
from jax.sharding import PartitionSpec as P

ZS = 8
MIB = 1024 * 1024


def shifted(block, axis, distance):
    count = lax.axis_size(axis)
    return lax.ppermute(block, axis, [(i, (i + distance) % count) for i in range(count)])


def passed_along(block, axis, distance):
    devices = range(lax.axis_size(axis))
    route = [(i - distance, i) for i in devices if i - distance in devices]
    return lax.ppermute(block, axis, route)


def params(mib):
    return pltpu.CompilerParams(vmem_limit_bytes=mib * MIB)


def norm_kernel(x_ref, g_ref, o_ref):
    x = x_ref[...].astype(jnp.float32)
    o_ref[...] = (
        x * lax.rsqrt(jnp.mean(x * x, axis=-1, keepdims=True) + 1e-05) * g_ref[...]
    ).astype(jnp.bfloat16)


def normalized(x, gain):
    return pl.pallas_call(
        norm_kernel,
        out_shape=jax.ShapeDtypeStruct(x.shape, jnp.bfloat16),
        compiler_params=params(16),
        cost_estimate=pl.CostEstimate(flops=0, bytes_accessed=2 * x.size * 2, transcendentals=0),
    )(x, gain)


def project_kernel(count, temp_ref, *refs):
    blocks, (wq_ref, wkv_ref, q_ref, kv_ref) = refs[:count], refs[count:]
    head_dim = wq_ref.shape[1]
    start = 0
    for block in blocks:
        rows = pl.ds(start, block.shape[0])
        start += block.shape[0]
        x = block[...]
        q = jnp.dot(x, wq_ref[...], preferred_element_type=jnp.float32)
        kv = jnp.dot(x, wkv_ref[...], preferred_element_type=jnp.float32)
        k = kv[:, :head_dim]
        q_scale = lax.rsqrt(jnp.mean(q * q, axis=-1, keepdims=True) + 1e-06)
        q_ref[rows, :] = (q * q_scale * temp_ref[0, 0] / head_dim).astype(jnp.bfloat16)
        k_scale = lax.rsqrt(jnp.mean(k * k, axis=-1, keepdims=True) + 1e-06)
        kv_ref[rows, :head_dim] = (k * k_scale).astype(jnp.bfloat16)
        kv_ref[rows, head_dim:] = kv[:, head_dim:].astype(jnp.bfloat16)


def projected(blocks, wq, wkv, temp):
    rows = sum(b.shape[0] for b in blocks)
    vmem = pl.BlockSpec(memory_space=pltpu.VMEM)
    return pl.pallas_call(
        functools.partial(project_kernel, len(blocks)),
        in_specs=[pl.BlockSpec(memory_space=pltpu.SMEM)] + [vmem] * (len(blocks) + 2),
        out_specs=[vmem, vmem],
        out_shape=[
            jax.ShapeDtypeStruct((rows, wq.shape[1]), jnp.bfloat16),
            jax.ShapeDtypeStruct((rows, wkv.shape[1]), jnp.bfloat16),
        ],
        compiler_params=params(32),
        cost_estimate=pl.CostEstimate(
            flops=2 * rows * 2048 * 384, bytes_accessed=rows * 5632 + 1572864, transcendentals=0
        ),
    )(temp, *blocks, wq, wkv)


def attend_kernel(sizes, at_ref, *refs):
    steps = len(sizes)
    q_refs, kv_refs = refs[:steps], refs[steps : 4 * steps]
    qpos_ref, qspan_ref, kpos_ref, o_ref, q_all, k_all, v_all, s_all = refs[4 * steps :]
    head_dim = q_all.shape[1]
    own_rows, keys = q_all.shape[0], k_all.shape[0]
    start = 0
    for step, size in enumerate(sizes):
        q_all[pl.ds(start, size), :] = q_refs[step][...]
        own, other, pair = kv_refs[3 * step : 3 * step + 3]
        for place, part in enumerate((own[...], other[...], pair[0], pair[1])):
            rows = pl.ds(place * own_rows + start, size)
            k_all[rows, :] = part[:, :head_dim]
            v_all[rows, :] = part[:, head_dim:]
        start += size
    tile, wide = 128, 512
    first_z = at_ref[0, 0]

    def one_block(b, _):
        rows = pl.ds(pl.multiple_of(b * tile, tile), tile)
        q = q_all[rows, :]
        qpos = jnp.broadcast_to(qpos_ref[rows, :], (tile, 128))
        qspan = jnp.broadcast_to(qspan_ref[rows, :], (tile, 128))
        peak = jnp.full((tile, 128), -1e30, jnp.float32)
        for t in range(keys // wide):
            s = lax.dot_general(
                q,
                k_all[t * wide : (t + 1) * wide, :],
                (((1,), (1,)), ((), ())),
                preferred_element_type=jnp.float32,
            )
            for u in range(wide // 128):
                lanes = slice(t * wide + u * 128, t * wide + (u + 1) * 128)
                back = qpos - kpos_ref[0:1, lanes]
                seen = (back >= 0) & (back <= qspan)
                part = jnp.where(seen, s[:, u * 128 : (u + 1) * 128], -1e30)
                s_all[:, lanes] = part
                peak = jnp.maximum(peak, part)
        top = jnp.max(peak, axis=-1, keepdims=True)
        total = jnp.zeros((tile, 128), jnp.float32)
        mixed = jnp.zeros((tile, head_dim), jnp.float32)
        for t in range(keys // wide):
            lanes = slice(t * wide, (t + 1) * wide)
            w = jnp.exp(s_all[:, lanes] - top)
            for u in range(wide // 128):
                total = total + w[:, u * 128 : (u + 1) * 128]
            mixed = mixed + jnp.dot(
                w.astype(jnp.bfloat16), v_all[lanes, :], preferred_element_type=jnp.float32
            )
        offset = lax.select(b == 0, 0, b)
        place = lax.rem(first_z + offset, ZS)
        o_ref[pl.ds(pl.multiple_of(place * tile, tile), tile), :] = (
            mixed / jnp.sum(total, axis=-1, keepdims=True)
        ).astype(jnp.bfloat16)
        return 0

    lax.fori_loop(0, own_rows // tile, one_block, 0)


def attended(at, queries, keyvals, qpos, qspan, kpos):
    sizes = tuple(q.shape[0] for q in queries)
    rows, keys, head_dim = sum(sizes), 4 * sum(sizes), queries[0].shape[1]
    vmem = pl.BlockSpec(memory_space=pltpu.VMEM)
    operands = [*queries, *[a for three in keyvals for a in three], qpos, qspan, kpos]
    return pl.pallas_call(
        functools.partial(attend_kernel, sizes),
        in_specs=[pl.BlockSpec(memory_space=pltpu.SMEM)] + [vmem] * len(operands),
        out_specs=vmem,
        out_shape=jax.ShapeDtypeStruct((rows, head_dim), jnp.bfloat16),
        scratch_shapes=[
            pltpu.VMEM((rows, head_dim), jnp.bfloat16),
            pltpu.VMEM((keys, head_dim), jnp.bfloat16),
            pltpu.VMEM((keys, head_dim), jnp.bfloat16),
            pltpu.VMEM((128, keys), jnp.float32),
        ],
        compiler_params=params(40),
        cost_estimate=pl.CostEstimate(
            flops=4 * rows * keys * head_dim, bytes_accessed=8 * keys * head_dim, transcendentals=rows * keys
        ),
    )(at, *operands)


def output_kernel(m_ref, w_ref, x_ref, o_ref):
    mixed = jnp.concatenate([m_ref[h] for h in range(m_ref.shape[0])], axis=1)
    wide = 512
    for t in range(w_ref.shape[1] // wide):
        lanes = slice(t * wide, (t + 1) * wide)
        added = jnp.dot(mixed, w_ref[:, lanes], preferred_element_type=jnp.float32)
        o_ref[:, lanes] = (x_ref[:, lanes].astype(jnp.float32) + added).astype(jnp.bfloat16)


def outputs(mixed, w_out, x):
    return pl.pallas_call(
        output_kernel,
        out_shape=jax.ShapeDtypeStruct(x.shape, jnp.bfloat16),
        compiler_params=params(24),
        cost_estimate=pl.CostEstimate(
            flops=2 * 128 * 1024 * 2048, bytes_accessed=6 * MIB, transcendentals=0
        ),
    )(mixed, w_out, x)


def per_device(acts, order, doc_ids, gain, w_query, w_keyval, w_out, head_temp):
    inputs = acts[0]
    width = w_query.shape[2]
    heads = head_temp.shape[1]
    head_dim = width // heads
    yh, z, c = (lax.axis_index(a) for a in ("yh", "z", "c"))

    normed = normalized(inputs, gain)

    slab = w_keyval[0]
    rows = slab.shape[0]
    by_head = jnp.concatenate(
        [slab[:, :width].reshape(rows, heads, head_dim), slab[:, width:].reshape(rows, heads, head_dim)], axis=2
    ).transpose(1, 0, 2)
    own_w = lax.all_to_all(by_head, "z", 0, 0, tiled=True)
    other_w = shifted(own_w, "yh", 1)
    both = jnp.stack([jnp.where(yh == 0, own_w, other_w), jnp.where(yh == 0, other_w, own_w)])
    across = shifted(both, "c", 1)
    wkv = jnp.stack(
        [jnp.where(c == 0, both, across), jnp.where(c == 0, across, both)], axis=2
    ).reshape(-1, 2 * head_dim)
    wq = lax.dynamic_slice_in_dim(w_query[0], z * head_dim, head_dim, axis=1)
    temp = lax.dynamic_slice_in_dim(head_temp, z, 1, axis=1)

    grid = order.reshape(2, ZS, 2, -1)
    grid = lax.dynamic_slice_in_dim(jnp.concatenate([grid, grid], axis=1), z, ZS, axis=1)
    grid = jnp.where(yh == 0, grid, grid[::-1])
    grid = jnp.where(c == 0, grid, grid[:, :, ::-1])
    qpos = grid[0, :, 0].reshape(-1, 1)
    begins = jnp.sum(
        (doc_ids[None, :] < jnp.arange(1, 8, dtype=jnp.int32)[:, None]).astype(jnp.int32), axis=1
    )
    began = jnp.max(jnp.where(begins[None, :] <= qpos, begins[None, :], 0), axis=1, keepdims=True)
    qspan = qpos - began
    kpos = grid.transpose(2, 0, 1, 3).reshape(1, -1)

    half = inputs.shape[0] // 2
    right, left = [normed], [normed]
    for _ in range(3):
        right.append(shifted(right[-1], "z", 1))
        left.append(shifted(left[-1], "z", -1))
    far_top = shifted(right[-1][:half], "z", 1)
    far_bottom = shifted(left[-1][half:], "z", -1)
    groups = [[normed, left[1]], [left[2], left[3]], [far_top, far_bottom], [right[3], right[2]], [right[1]]]
    groups = [[normed], [left[1]], [left[2]], [left[3]], [far_top, far_bottom], [right[3]], [right[2]], [right[1]]]
    queries, keyvals = [None] * 8, [None] * 8
    for g in (0, 1, 7, 2, 6, 3, 5, 4):
        q, kv = projected(groups[g], wq, wkv, temp)
        other = shifted(kv, "yh", 1)
        pair = shifted(jnp.stack([kv, other]), "c", 1)
        queries[g], keyvals[g] = q, (kv, other, pair)

    at = z.astype(jnp.int32).reshape(1, 1)
    mixed = attended(at, queries, keyvals, qpos, qspan, kpos)
    mixed = lax.all_to_all(mixed.reshape(ZS, -1, head_dim), "z", 0, 0, tiled=True)
    produced = outputs(mixed, w_out[0], inputs)
    handed = passed_along(produced, ("yl", "x"), 1)
    return (produced[None], handed[None])


def solution(mesh):
    devices = np.asarray(mesh.devices).reshape(2, ZS, 2, 2, 4)
    fine = Mesh(devices, ("yh", "z", "c", "yl", "x"))
    phase, blk = ("yl", "x"), ("yh", "z", "c")
    return jax.shard_map(
        per_device,
        mesh=fine,
        in_specs=(
            P(phase, blk, None),
            P(),
            P(),
            P(phase, None),
            P(phase, None, None),
            P(phase, blk, None),
            P(phase, None, None),
            P(phase, None),
        ),
        out_specs=(P(phase, blk, None), P(phase, blk, None)),
        check_vma=False,
    )
```

```python
import functools

import jax
import jax.numpy as jnp
import numpy as np
from jax import lax
from jax.experimental import pallas as pl
from jax.experimental.pallas import tpu as pltpu
from jax.sharding import Mesh
from jax.sharding import PartitionSpec as P

ZS = 8
EARLY, LATE = (0, 1, 7, 2, 6), (3, 5, 4)
MIB = 1024 * 1024


def shifted(block, axis, distance):
    count = lax.axis_size(axis)
    return lax.ppermute(block, axis, [(i, (i + distance) % count) for i in range(count)])


def passed_along(block, axis, distance):
    devices = range(lax.axis_size(axis))
    route = [(i - distance, i) for i in devices if i - distance in devices]
    return lax.ppermute(block, axis, route)


def params(mib):
    return pltpu.CompilerParams(vmem_limit_bytes=mib * MIB)


def entry_kernel(x_ref, g_ref, w_ref, upper_ref, lower_ref, p_ref):
    half = upper_ref.shape[0]
    for part, n_ref in enumerate((upper_ref, lower_ref)):
        x = x_ref[part * half : (part + 1) * half, :].astype(jnp.float32)
        n_ref[...] = (
            x * lax.rsqrt(jnp.mean(x * x, axis=-1, keepdims=True) + 1e-05) * g_ref[...]
        ).astype(jnp.bfloat16)
    heads, _, wide = p_ref.shape
    width, head_dim = heads * wide // 2, wide // 2
    for h in range(heads):
        p_ref[h, :, :head_dim] = w_ref[:, h * head_dim : (h + 1) * head_dim]
        p_ref[h, :, head_dim:] = w_ref[:, width + h * head_dim : width + (h + 1) * head_dim]


def entry(x, gain, slab, heads):
    rows, columns = slab.shape
    return pl.pallas_call(
        entry_kernel,
        out_shape=[
            *[jax.ShapeDtypeStruct((x.shape[0] // 2, x.shape[1]), jnp.bfloat16)] * 2,
            jax.ShapeDtypeStruct((heads, rows, columns // heads), jnp.bfloat16),
        ],
        compiler_params=params(16),
        cost_estimate=pl.CostEstimate(flops=0, bytes_accessed=3 * x.size * 2, transcendentals=0),
    )(x, gain, slab)


def assemble_kernel(at_ref, own, across, over, both, w_ref):
    rings, rows, _ = own.shape
    yh, core = at_ref[0], at_ref[1]
    for place, part in enumerate((own, across, over, both)):
        half, side = yh ^ (place // 2), core ^ (place % 2)
        for z in range(rings):
            start = half * (2 * rings * rows) + side * rows + z * 2 * rows
            w_ref[pl.ds(pl.multiple_of(start, rows), rows), :] = part[z]


def assembled(at, *parts):
    rings, rows, columns = parts[0].shape
    vmem = pl.BlockSpec(memory_space=pltpu.VMEM)
    return pl.pallas_call(
        assemble_kernel,
        in_specs=[pl.BlockSpec(memory_space=pltpu.SMEM)] + [vmem] * 4,
        out_specs=vmem,
        out_shape=jax.ShapeDtypeStruct((4 * rings * rows, columns), jnp.bfloat16),
        compiler_params=params(16),
        cost_estimate=pl.CostEstimate(flops=0, bytes_accessed=2 * MIB, transcendentals=0),
    )(at, *parts)


def project_kernel(count, temp_ref, *refs):
    blocks, (wq_ref, wkv_ref, q_ref, kv_ref) = refs[:count], refs[count:]
    head_dim = wq_ref.shape[1]
    x = jnp.concatenate([block[...] for block in blocks], axis=0)
    q = jnp.dot(x, wq_ref[...], preferred_element_type=jnp.float32)
    kv = jnp.dot(x, wkv_ref[...], preferred_element_type=jnp.float32)
    k = kv[:, :head_dim]
    q_scale = lax.rsqrt(jnp.mean(q * q, axis=-1, keepdims=True) + 1e-06)
    q_ref[...] = (q * q_scale * temp_ref[0, 0] / head_dim).astype(jnp.bfloat16)
    k_scale = lax.rsqrt(jnp.mean(k * k, axis=-1, keepdims=True) + 1e-06)
    kv_ref[:, :head_dim] = (k * k_scale).astype(jnp.bfloat16)
    kv_ref[:, head_dim:] = kv[:, head_dim:].astype(jnp.bfloat16)


def projected(blocks, wq, wkv, temp):
    rows = sum(b.shape[0] for b in blocks)
    vmem = pl.BlockSpec(memory_space=pltpu.VMEM)
    return pl.pallas_call(
        functools.partial(project_kernel, len(blocks)),
        in_specs=[pl.BlockSpec(memory_space=pltpu.SMEM)] + [vmem] * (len(blocks) + 2),
        out_specs=[vmem, vmem],
        out_shape=[
            jax.ShapeDtypeStruct((rows, wq.shape[1]), jnp.bfloat16),
            jax.ShapeDtypeStruct((rows, wkv.shape[1]), jnp.bfloat16),
        ],
        compiler_params=params(32),
        cost_estimate=pl.CostEstimate(
            flops=2 * rows * 2048 * 384, bytes_accessed=rows * 5632 + 1572864, transcendentals=0
        ),
    )(temp, *blocks, wq, wkv)


def masked_scores(q, keyval, places, qpos, qspan, s_all, column, peak):
    head_dim = q.shape[1]
    s = lax.dot_general(
        q, keyval[:, :head_dim], (((1,), (1,)), ((), ())), preferred_element_type=jnp.float32
    )
    for u, place in enumerate(places):
        lanes = slice(u * 128, (u + 1) * 128)
        part = jnp.where(qpos - place <= qspan, s[:, lanes], -1e30)
        s_all[:, column + u * 128 : column + (u + 1) * 128] = part
        peak = jnp.maximum(peak, part)
    return peak


def mixing(s_all, column, keyval, top, total, mixed):
    rows, head_dim = keyval.shape[0], keyval.shape[1] // 2
    parts = []
    for u in range(rows // 128):
        w = jnp.exp(s_all[:, column + u * 128 : column + (u + 1) * 128] - top)
        total = total + w
        parts.append(w.astype(jnp.bfloat16))
    w = jnp.concatenate(parts, axis=1)
    return total, mixed + jnp.dot(w, keyval[:, head_dim:], preferred_element_type=jnp.float32)


def chunks(segments, kpos_ref, most=512):
    column = 0
    for keyval, place, offsets in segments:
        for start in range(0, keyval.shape[0], most):
            size = min(most, keyval.shape[0] - start)
            places = [
                kpos_ref[place : place + 1, o * 128 : (o + 1) * 128]
                for o in offsets[start // 128 : (start + size) // 128]
            ]
            yield column, keyval, slice(start, start + size), places
            column += size


TILE = 256


def tile_of(t, at_ref, qpos_ref, qspan_ref):
    qpos, qspan = [], []
    for i in range(TILE // 128):
        placed = pl.ds(pl.multiple_of(at_ref[0, t * (TILE // 128) + i] * 128, 128), 128)
        qpos.append(jnp.broadcast_to(qpos_ref[placed, :], (128, 128)))
        qspan.append(jnp.broadcast_to(qspan_ref[placed, :], (128, 128)))
    rows = pl.ds(pl.multiple_of(t * TILE, TILE), TILE)
    return rows, jnp.concatenate(qpos, axis=0), jnp.concatenate(qspan, axis=0)


def weighed(q, peak, segments, kpos_ref, qpos, qspan, s_all):
    for column, keyval, cut, places in chunks(segments, kpos_ref):
        peak = masked_scores(q, keyval[cut, :], places, qpos, qspan, s_all, column, peak)
    top = jnp.broadcast_to(jnp.max(peak, axis=-1, keepdims=True), peak.shape)
    total = jnp.zeros((TILE, 128), jnp.float32)
    mixed = jnp.zeros((TILE, q.shape[1]), jnp.float32)
    for column, keyval, cut, _ in chunks(segments, kpos_ref):
        total, mixed = mixing(s_all, column, keyval[cut, :], top, total, mixed)
    return top, total, mixed


def first_kernel(at_ref, qa, qb, own_a, own_b, ca, ya, xa, qpos_ref, qspan_ref, kpos_ref, q_out, acc, top_out, total_out, s_all):
    early, late = qa.shape[0], qb.shape[0]
    q_out[pl.ds(0, early), :] = qa[...]
    q_out[pl.ds(early, late), :] = qb[...]
    segments = [(own_a, 0, EARLY), (own_b, 0, LATE)]
    segments += [(ca, 1, EARLY), (ya, 2, EARLY), (xa, 3, EARLY)]

    def one_tile(t, _):
        rows, qpos, qspan = tile_of(t, at_ref, qpos_ref, qspan_ref)
        peak = jnp.full((TILE, 128), -1e30, jnp.float32)
        top, total, mixed = weighed(q_out[rows, :], peak, segments, kpos_ref, qpos, qspan, s_all)
        acc[rows, :] = mixed
        total_out[rows, :] = total
        top_out[rows, :] = top
        return 0

    lax.fori_loop(0, (early + late) // TILE, one_tile, 0)


def second_kernel(at_ref, q_ref, acc, top_ref, total_ref, cb, yb, xb, qpos_ref, qspan_ref, kpos_ref, o_ref, s_all):
    segments = [(cb, 1, LATE), (yb, 2, LATE), (xb, 3, LATE)]

    def one_tile(t, _):
        rows, qpos, qspan = tile_of(t, at_ref, qpos_ref, qspan_ref)
        before = top_ref[rows, :]
        top, total, mixed = weighed(q_ref[rows, :], before, segments, kpos_ref, qpos, qspan, s_all)
        kept = jnp.exp(before - top)
        summed = acc[rows, :] * kept + mixed
        weight = jnp.sum(total_ref[rows, :] * kept + total, axis=-1, keepdims=True)
        result = (summed / weight).astype(jnp.bfloat16)
        for i in range(TILE // 128):
            placed = pl.ds(pl.multiple_of(at_ref[1, t * (TILE // 128) + i] * 128, 128), 128)
            o_ref[placed, :] = result[i * 128 : (i + 1) * 128, :]
        return 0

    lax.fori_loop(0, q_ref.shape[0] // TILE, one_tile, 0)


def attended_first(at, queries, own, others, qpos, qspan, kpos):
    early, late = (q.shape[0] for q in queries)
    rows, head_dim = early + late, queries[0].shape[1]
    keys = rows + 3 * early
    wide = jax.ShapeDtypeStruct((rows, head_dim), jnp.float32)
    vmem = pl.BlockSpec(memory_space=pltpu.VMEM)
    return pl.pallas_call(
        first_kernel,
        in_specs=[pl.BlockSpec(memory_space=pltpu.SMEM)] + [vmem] * 10,
        out_specs=[vmem] * 4,
        out_shape=[jax.ShapeDtypeStruct((rows, head_dim), jnp.bfloat16), wide, wide, wide],
        scratch_shapes=[pltpu.VMEM((TILE, keys), jnp.float32)],
        compiler_params=params(24),
        cost_estimate=pl.CostEstimate(
            flops=40 * rows * keys * head_dim, bytes_accessed=4 * keys * head_dim, transcendentals=rows * keys
        ),
    )(at, *queries, *own, *others, qpos, qspan, kpos)


def attended_second(at, state, others, qpos, qspan, kpos):
    rows, head_dim = state[0].shape
    keys = 3 * others[0].shape[0]
    vmem = pl.BlockSpec(memory_space=pltpu.VMEM)
    return pl.pallas_call(
        second_kernel,
        in_specs=[pl.BlockSpec(memory_space=pltpu.SMEM)] + [vmem] * 10,
        out_specs=vmem,
        out_shape=jax.ShapeDtypeStruct((rows, head_dim), jnp.bfloat16),
        scratch_shapes=[pltpu.VMEM((TILE, keys), jnp.float32)],
        compiler_params=params(24),
        cost_estimate=pl.CostEstimate(
            flops=40 * rows * keys * head_dim, bytes_accessed=4 * keys * head_dim, transcendentals=rows * keys
        ),
    )(at, *state, *others, qpos, qspan, kpos)


def output_kernel(m_ref, w_ref, x_ref, o_ref):
    mixed = jnp.concatenate([m_ref[h] for h in range(m_ref.shape[0])], axis=1)
    wide = 512
    for t in range(w_ref.shape[1] // wide):
        lanes = slice(t * wide, (t + 1) * wide)
        added = jnp.dot(mixed, w_ref[:, lanes], preferred_element_type=jnp.float32)
        o_ref[:, lanes] = (x_ref[:, lanes].astype(jnp.float32) + added).astype(jnp.bfloat16)


def outputs(mixed, w_out, x):
    return pl.pallas_call(
        output_kernel,
        out_shape=jax.ShapeDtypeStruct(x.shape, jnp.bfloat16),
        compiler_params=params(24),
        cost_estimate=pl.CostEstimate(
            flops=2 * 128 * 1024 * 2048, bytes_accessed=6 * MIB, transcendentals=0
        ),
    )(mixed, w_out, x)


def per_device(acts, order, doc_ids, gain, w_query, w_keyval, w_out, head_temp):
    inputs = acts[0]
    width = w_query.shape[2]
    heads = head_temp.shape[1]
    head_dim = width // heads
    yh, z, c = (lax.axis_index(a).astype(jnp.int32) for a in ("yh", "z", "c"))

    upper, lower, by_head = entry(inputs, gain, w_keyval[0], heads)

    blocks = {(0, 0): upper, (0, 1): lower}
    for distance in (1, 2, 3):
        for part in (0, 1):
            blocks[-distance, part] = shifted(blocks[1 - distance, part], "z", 1)
            blocks[distance, part] = shifted(blocks[distance - 1, part], "z", -1)
    blocks[4, 0] = shifted(blocks[-3, 0], "z", 1)
    blocks[4, 1] = shifted(blocks[3, 1], "z", -1)

    def rows_of(offset):
        at_offset = offset if offset <= 4 else offset - ZS
        return [blocks[at_offset, 0], blocks[at_offset, 1]]

    own_w = lax.all_to_all(by_head, "z", 0, 0, tiled=True)
    other_w = shifted(own_w, "yh", 1)
    wkv = assembled(jnp.stack([yh, c]), own_w, shifted(own_w, "c", 1), other_w, shifted(other_w, "c", 1))
    wq = lax.dynamic_slice_in_dim(w_query[0], z * head_dim, head_dim, axis=1)
    temp = lax.dynamic_slice_in_dim(head_temp, z, 1, axis=1)

    grid = order.reshape(2, ZS, 2, -1)
    grid = lax.dynamic_slice_in_dim(jnp.concatenate([grid, grid], axis=1), z, ZS, axis=1)
    grid = jnp.where(yh == 0, grid, grid[::-1])
    grid = jnp.where(c == 0, grid, grid[:, :, ::-1])
    kpos = grid.transpose(0, 2, 1, 3).reshape(4, -1)
    begins = jnp.sum(
        (doc_ids[None, :] < jnp.arange(1, 8, dtype=jnp.int32)[:, None]).astype(jnp.int32), axis=1
    )
    own_pos = kpos[0].reshape(-1, 1)
    began = jnp.max(jnp.where(begins[None, :] <= own_pos, begins[None, :], 0), axis=1, keepdims=True)
    lowest = jnp.int32(-(2**31))
    qspan = own_pos - began + lowest
    qpos = own_pos + lowest

    q_early, kv_early = projected(sum([rows_of(o) for o in EARLY], []), wq, wkv, temp)
    q_late, kv_late = projected(sum([rows_of(o) for o in LATE], []), wq, wkv, temp)
    over_early = shifted(kv_early, "yh", 1)
    kv_late, over_later = lax.optimization_barrier((kv_late, over_early))
    others_early = [shifted(kv_early, "c", 1), over_early, shifted(over_later, "c", 1)]
    others_late = [lax.ppermute(kv_late, ("yh", "c"), [(i, i ^ k) for i in range(4)]) for k in (1, 2, 3)]
    offsets = jnp.array(EARLY + LATE, jnp.int32)
    at = jnp.stack([offsets, lax.rem(z + offsets, ZS)])
    state = attended_first(at, [q_early, q_late], [kv_early, kv_late], others_early, qpos, qspan, kpos)
    mixed = attended_second(at, state, others_late, qpos, qspan, kpos)

    mixed = lax.all_to_all(mixed.reshape(ZS, -1, head_dim), "z", 0, 0, tiled=True)
    produced = outputs(mixed, w_out[0], inputs)
    handed = passed_along(produced, ("yl", "x"), 1)
    return (produced[None], handed[None])


def solution(mesh):
    devices = np.asarray(mesh.devices).reshape(2, ZS, 2, 2, 4)
    fine = Mesh(devices, ("yh", "z", "c", "yl", "x"))
    phase, blk = ("yl", "x"), ("yh", "z", "c")
    return jax.shard_map(
        per_device,
        mesh=fine,
        in_specs=(
            P(phase, blk, None),
            P(),
            P(),
            P(phase, None),
            P(phase, None, None),
            P(phase, blk, None),
            P(phase, None, None),
            P(phase, None),
        ),
        out_specs=(P(phase, blk, None), P(phase, blk, None)),
        check_vma=False,
    )
```

```python
import functools

import jax
import jax.numpy as jnp
import numpy as np
from jax import lax
from jax.experimental import pallas as pl
from jax.experimental.pallas import tpu as pltpu
from jax.sharding import Mesh
from jax.sharding import PartitionSpec as P

ZS = 8
EARLY, LATE = (0, 1, 7, 2, 6), (3, 5, 4)
MIB = 1024 * 1024


def shifted(block, axis, distance):
    count = lax.axis_size(axis)
    return lax.ppermute(block, axis, [(i, (i + distance) % count) for i in range(count)])


def passed_along(block, axis, distance):
    devices = range(lax.axis_size(axis))
    route = [(i - distance, i) for i in devices if i - distance in devices]
    return lax.ppermute(block, axis, route)


def params(mib):
    return pltpu.CompilerParams(vmem_limit_bytes=mib * MIB)


def entry_kernel(x_ref, g_ref, w_ref, upper_ref, lower_ref, p_ref):
    half = upper_ref.shape[0]
    for part, n_ref in enumerate((upper_ref, lower_ref)):
        x = x_ref[part * half : (part + 1) * half, :].astype(jnp.float32)
        n_ref[...] = (
            x * lax.rsqrt(jnp.mean(x * x, axis=-1, keepdims=True) + 1e-05) * g_ref[...]
        ).astype(jnp.bfloat16)
    heads, _, wide = p_ref.shape
    width, head_dim = heads * wide // 2, wide // 2
    for h in range(heads):
        p_ref[h, :, :head_dim] = w_ref[:, h * head_dim : (h + 1) * head_dim]
        p_ref[h, :, head_dim:] = w_ref[:, width + h * head_dim : width + (h + 1) * head_dim]


def entry(x, gain, slab, heads):
    rows, columns = slab.shape
    return pl.pallas_call(
        entry_kernel,
        out_shape=[
            *[jax.ShapeDtypeStruct((x.shape[0] // 2, x.shape[1]), jnp.bfloat16)] * 2,
            jax.ShapeDtypeStruct((heads, rows, columns // heads), jnp.bfloat16),
        ],
        compiler_params=params(16),
        cost_estimate=pl.CostEstimate(flops=0, bytes_accessed=3 * x.size * 2, transcendentals=0),
    )(x, gain, slab)


def assemble_kernel(at_ref, own, across, over, both, w_ref):
    rings, rows, _ = own.shape
    yh, core = at_ref[0], at_ref[1]
    for place, part in enumerate((own, across, over, both)):
        half, side = yh ^ (place // 2), core ^ (place % 2)
        for z in range(rings):
            start = half * (2 * rings * rows) + side * rows + z * 2 * rows
            w_ref[pl.ds(pl.multiple_of(start, rows), rows), :] = part[z]


def assembled(at, *parts):
    rings, rows, columns = parts[0].shape
    vmem = pl.BlockSpec(memory_space=pltpu.VMEM)
    return pl.pallas_call(
        assemble_kernel,
        in_specs=[pl.BlockSpec(memory_space=pltpu.SMEM)] + [vmem] * 4,
        out_specs=vmem,
        out_shape=jax.ShapeDtypeStruct((4 * rings * rows, columns), jnp.bfloat16),
        compiler_params=params(16),
        cost_estimate=pl.CostEstimate(flops=0, bytes_accessed=2 * MIB, transcendentals=0),
    )(at, *parts)


def project_kernel(count, temp_ref, *refs):
    blocks, (wq_ref, wkv_ref, q_ref, kv_ref) = refs[:count], refs[count:]
    head_dim = wq_ref.shape[1]
    x = jnp.concatenate([block[...] for block in blocks], axis=0)
    q = jnp.dot(x, wq_ref[...], preferred_element_type=jnp.float32)
    kv = jnp.dot(x, wkv_ref[...], preferred_element_type=jnp.float32)
    k = kv[:, :head_dim]
    q_scale = lax.rsqrt(jnp.mean(q * q, axis=-1, keepdims=True) + 1e-06)
    q_ref[...] = (q * q_scale * temp_ref[0, 0] / head_dim).astype(jnp.bfloat16)
    k_scale = lax.rsqrt(jnp.mean(k * k, axis=-1, keepdims=True) + 1e-06)
    kv_ref[:, :head_dim] = (k * k_scale).astype(jnp.bfloat16)
    kv_ref[:, head_dim:] = kv[:, head_dim:].astype(jnp.bfloat16)


def projected(blocks, wq, wkv, temp):
    rows = sum(b.shape[0] for b in blocks)
    vmem = pl.BlockSpec(memory_space=pltpu.VMEM)
    return pl.pallas_call(
        functools.partial(project_kernel, len(blocks)),
        in_specs=[pl.BlockSpec(memory_space=pltpu.SMEM)] + [vmem] * (len(blocks) + 2),
        out_specs=[vmem, vmem],
        out_shape=[
            jax.ShapeDtypeStruct((rows, wq.shape[1]), jnp.bfloat16),
            jax.ShapeDtypeStruct((rows, wkv.shape[1]), jnp.bfloat16),
        ],
        compiler_params=params(32),
        cost_estimate=pl.CostEstimate(
            flops=2 * rows * 2048 * 384, bytes_accessed=rows * 5632 + 1572864, transcendentals=0
        ),
    )(temp, *blocks, wq, wkv)


def masked_scores(q, keyval, places, qpos, qspan, s_all, column, peak):
    head_dim = q.shape[1]
    s = lax.dot_general(
        q, keyval[:, :head_dim], (((1,), (1,)), ((), ())), preferred_element_type=jnp.float32
    )
    for u, place in enumerate(places):
        lanes = slice(u * 128, (u + 1) * 128)
        part = jnp.where(qpos - place <= qspan, s[:, lanes], -1e30)
        s_all[:, column + u * 128 : column + (u + 1) * 128] = part
        peak = jnp.maximum(peak, part)
    return peak


def mixing(s_all, column, keyval, top, total, mixed):
    rows, head_dim = keyval.shape[0], keyval.shape[1] // 2
    parts = []
    for u in range(rows // 128):
        w = jnp.exp(s_all[:, column + u * 128 : column + (u + 1) * 128] - top)
        total = total + w
        parts.append(w.astype(jnp.bfloat16))
    w = jnp.concatenate(parts, axis=1)
    return total, mixed + jnp.dot(w, keyval[:, head_dim:], preferred_element_type=jnp.float32)


def chunks(segments, kpos_ref, most=512):
    column = 0
    for keyval, place, offsets in segments:
        for start in range(0, keyval.shape[0], most):
            size = min(most, keyval.shape[0] - start)
            places = [
                kpos_ref[place : place + 1, o * 128 : (o + 1) * 128]
                for o in offsets[start // 128 : (start + size) // 128]
            ]
            yield column, keyval, slice(start, start + size), places
            column += size


TILE = 256


def tile_of(t, at_ref, qpos_ref, qspan_ref):
    qpos, qspan = [], []
    for i in range(TILE // 128):
        placed = pl.ds(pl.multiple_of(at_ref[0, t * (TILE // 128) + i] * 128, 128), 128)
        qpos.append(jnp.broadcast_to(qpos_ref[placed, :], (128, 128)))
        qspan.append(jnp.broadcast_to(qspan_ref[placed, :], (128, 128)))
    rows = pl.ds(pl.multiple_of(t * TILE, TILE), TILE)
    return rows, jnp.concatenate(qpos, axis=0), jnp.concatenate(qspan, axis=0)


def weighed(q, peak, segments, kpos_ref, qpos, qspan, s_all):
    for column, keyval, cut, places in chunks(segments, kpos_ref):
        peak = masked_scores(q, keyval[cut, :], places, qpos, qspan, s_all, column, peak)
    top = jnp.broadcast_to(jnp.max(peak, axis=-1, keepdims=True), peak.shape)
    total = jnp.zeros((TILE, 128), jnp.float32)
    mixed = jnp.zeros((TILE, q.shape[1]), jnp.float32)
    for column, keyval, cut, _ in chunks(segments, kpos_ref):
        total, mixed = mixing(s_all, column, keyval[cut, :], top, total, mixed)
    return top, total, mixed


def attend_kernel(at_ref, qa, qb, *refs):
    parts, (qpos_ref, qspan_ref, kpos_ref, o_ref, q_all, s_all) = refs[:8], refs[8:]
    early, late = qa.shape[0], qb.shape[0]
    q_all[pl.ds(0, early), :] = qa[...]
    q_all[pl.ds(early, late), :] = qb[...]
    segments = [(parts[i], i, EARLY) for i in range(4)] + [(parts[4 + i], i, LATE) for i in range(4)]

    def one_tile(t, _):
        rows, qpos, qspan = tile_of(t, at_ref, qpos_ref, qspan_ref)
        peak = jnp.full((TILE, 128), -1e30, jnp.float32)
        _, total, mixed = weighed(q_all[rows, :], peak, segments, kpos_ref, qpos, qspan, s_all)
        result = (mixed / jnp.sum(total, axis=-1, keepdims=True)).astype(jnp.bfloat16)
        for i in range(TILE // 128):
            placed = pl.ds(pl.multiple_of(at_ref[1, t * (TILE // 128) + i] * 128, 128), 128)
            o_ref[placed, :] = result[i * 128 : (i + 1) * 128, :]
        return 0

    lax.fori_loop(0, (early + late) // TILE, one_tile, 0)


def attended(at, queries, keyvals, qpos, qspan, kpos):
    rows, head_dim = sum(q.shape[0] for q in queries), queries[0].shape[1]
    keys = sum(k.shape[0] for k in keyvals)
    vmem = pl.BlockSpec(memory_space=pltpu.VMEM)
    return pl.pallas_call(
        attend_kernel,
        in_specs=[pl.BlockSpec(memory_space=pltpu.SMEM)] + [vmem] * 13,
        out_specs=vmem,
        out_shape=jax.ShapeDtypeStruct((rows, head_dim), jnp.bfloat16),
        scratch_shapes=[
            pltpu.VMEM((rows, head_dim), jnp.bfloat16),
            pltpu.VMEM((TILE, keys), jnp.float32),
        ],
        compiler_params=params(24),
        cost_estimate=pl.CostEstimate(
            flops=40 * rows * keys * head_dim, bytes_accessed=4 * keys * head_dim, transcendentals=rows * keys
        ),
    )(at, *queries, *keyvals, qpos, qspan, kpos)


def output_kernel(m_ref, w_ref, x_ref, o_ref):
    mixed = jnp.concatenate([m_ref[h] for h in range(m_ref.shape[0])], axis=1)
    wide = 512
    for t in range(w_ref.shape[1] // wide):
        lanes = slice(t * wide, (t + 1) * wide)
        added = jnp.dot(mixed, w_ref[:, lanes], preferred_element_type=jnp.float32)
        o_ref[:, lanes] = (x_ref[:, lanes].astype(jnp.float32) + added).astype(jnp.bfloat16)


def outputs(mixed, w_out, x):
    return pl.pallas_call(
        output_kernel,
        out_shape=jax.ShapeDtypeStruct(x.shape, jnp.bfloat16),
        compiler_params=params(24),
        cost_estimate=pl.CostEstimate(
            flops=2 * 128 * 1024 * 2048, bytes_accessed=6 * MIB, transcendentals=0
        ),
    )(mixed, w_out, x)


def per_device(acts, order, doc_ids, gain, w_query, w_keyval, w_out, head_temp):
    inputs = acts[0]
    width = w_query.shape[2]
    heads = head_temp.shape[1]
    head_dim = width // heads
    yh, z, c = (lax.axis_index(a).astype(jnp.int32) for a in ("yh", "z", "c"))

    upper, lower, by_head = entry(inputs, gain, w_keyval[0], heads)

    blocks = {(0, 0): upper, (0, 1): lower}
    for distance in (1, 2, 3):
        for part in (0, 1):
            blocks[-distance, part] = shifted(blocks[1 - distance, part], "z", 1)
            blocks[distance, part] = shifted(blocks[distance - 1, part], "z", -1)
    blocks[4, 0] = shifted(blocks[-3, 0], "z", 1)
    blocks[4, 1] = shifted(blocks[3, 1], "z", -1)

    def rows_of(offset):
        at_offset = offset if offset <= 4 else offset - ZS
        return [blocks[at_offset, 0], blocks[at_offset, 1]]

    own_w = lax.all_to_all(by_head, "z", 0, 0, tiled=True)
    other_w = shifted(own_w, "yh", 1)
    wkv = assembled(jnp.stack([yh, c]), own_w, shifted(own_w, "c", 1), other_w, shifted(other_w, "c", 1))
    wq = lax.dynamic_slice_in_dim(w_query[0], z * head_dim, head_dim, axis=1)
    temp = lax.dynamic_slice_in_dim(head_temp, z, 1, axis=1)

    grid = order.reshape(2, ZS, 2, -1)
    grid = lax.dynamic_slice_in_dim(jnp.concatenate([grid, grid], axis=1), z, ZS, axis=1)
    grid = jnp.where(yh == 0, grid, grid[::-1])
    grid = jnp.where(c == 0, grid, grid[:, :, ::-1])
    kpos = grid.transpose(0, 2, 1, 3).reshape(4, -1)
    begins = jnp.sum(
        (doc_ids[None, :] < jnp.arange(1, 8, dtype=jnp.int32)[:, None]).astype(jnp.int32), axis=1
    )
    own_pos = kpos[0].reshape(-1, 1)
    began = jnp.max(jnp.where(begins[None, :] <= own_pos, begins[None, :], 0), axis=1, keepdims=True)
    lowest = jnp.int32(-(2**31))
    qspan = own_pos - began + lowest
    qpos = own_pos + lowest

    q_early, kv_early = projected(sum([rows_of(o) for o in EARLY], []), wq, wkv, temp)
    q_late, kv_late = projected(sum([rows_of(o) for o in LATE], []), wq, wkv, temp)
    over_early = shifted(kv_early, "yh", 1)
    _, over_later = lax.optimization_barrier((kv_late, over_early))
    over_late = shifted(kv_late, "yh", 1)
    keyvals = [kv_early, shifted(kv_early, "c", 1), over_early, shifted(over_later, "c", 1)]
    keyvals += [kv_late, shifted(kv_late, "c", 1), over_late, shifted(over_late, "c", 1)]
    offsets = jnp.array(EARLY + LATE, jnp.int32)
    at = jnp.stack([offsets, lax.rem(z + offsets, ZS)])
    mixed = attended(at, [q_early, q_late], keyvals, qpos, qspan, kpos)

    mixed = lax.all_to_all(mixed.reshape(ZS, -1, head_dim), "z", 0, 0, tiled=True)
    produced = outputs(mixed, w_out[0], inputs)
    handed = passed_along(produced, ("yl", "x"), 1)
    return (produced[None], handed[None])


def solution(mesh):
    devices = np.asarray(mesh.devices).reshape(2, ZS, 2, 2, 4)
    fine = Mesh(devices, ("yh", "z", "c", "yl", "x"))
    phase, blk = ("yl", "x"), ("yh", "z", "c")
    return jax.shard_map(
        per_device,
        mesh=fine,
        in_specs=(
            P(phase, blk, None),
            P(),
            P(),
            P(phase, None),
            P(phase, None, None),
            P(phase, blk, None),
            P(phase, None, None),
            P(phase, None),
        ),
        out_specs=(P(phase, blk, None), P(phase, blk, None)),
        check_vma=False,
    )
```

```python
import functools

import jax
import jax.numpy as jnp
import numpy as np
from jax import lax
from jax.experimental import pallas as pl
from jax.experimental.pallas import tpu as pltpu
from jax.sharding import Mesh
from jax.sharding import PartitionSpec as P

ZS = 8
EARLY, LATE = (0, 1, 7, 2, 6), (3, 5, 4)
MIB = 1024 * 1024


def shifted(block, axis, distance):
    count = lax.axis_size(axis)
    return lax.ppermute(block, axis, [(i, (i + distance) % count) for i in range(count)])


def passed_along(block, axis, distance):
    devices = range(lax.axis_size(axis))
    route = [(i - distance, i) for i in devices if i - distance in devices]
    return lax.ppermute(block, axis, route)


def params(mib):
    return pltpu.CompilerParams(vmem_limit_bytes=mib * MIB)


def entry_kernel(x_ref, g_ref, w_ref, upper_ref, lower_ref, p_ref):
    half = upper_ref.shape[0]
    for part, n_ref in enumerate((upper_ref, lower_ref)):
        x = x_ref[part * half : (part + 1) * half, :].astype(jnp.float32)
        n_ref[...] = (
            x * lax.rsqrt(jnp.mean(x * x, axis=-1, keepdims=True) + 1e-05) * g_ref[...]
        ).astype(jnp.bfloat16)
    heads, _, wide = p_ref.shape
    width, head_dim = heads * wide // 2, wide // 2
    for h in range(heads):
        p_ref[h, :, :head_dim] = w_ref[:, h * head_dim : (h + 1) * head_dim]
        p_ref[h, :, head_dim:] = w_ref[:, width + h * head_dim : width + (h + 1) * head_dim]


def entry(x, gain, slab, heads):
    rows, columns = slab.shape
    return pl.pallas_call(
        entry_kernel,
        out_shape=[
            *[jax.ShapeDtypeStruct((x.shape[0] // 2, x.shape[1]), jnp.bfloat16)] * 2,
            jax.ShapeDtypeStruct((heads, rows, columns // heads), jnp.bfloat16),
        ],
        compiler_params=params(16),
        cost_estimate=pl.CostEstimate(flops=0, bytes_accessed=3 * x.size * 2, transcendentals=0),
    )(x, gain, slab)


def assemble_kernel(at_ref, own, across, over, both, w_ref):
    rings, rows, _ = own.shape
    yh, core = at_ref[0], at_ref[1]
    for place, part in enumerate((own, across, over, both)):
        half, side = yh ^ (place // 2), core ^ (place % 2)
        for z in range(rings):
            start = half * (2 * rings * rows) + side * rows + z * 2 * rows
            w_ref[pl.ds(pl.multiple_of(start, rows), rows), :] = part[z]


def assembled(at, *parts):
    rings, rows, columns = parts[0].shape
    vmem = pl.BlockSpec(memory_space=pltpu.VMEM)
    return pl.pallas_call(
        assemble_kernel,
        in_specs=[pl.BlockSpec(memory_space=pltpu.SMEM)] + [vmem] * 4,
        out_specs=vmem,
        out_shape=jax.ShapeDtypeStruct((4 * rings * rows, columns), jnp.bfloat16),
        compiler_params=params(16),
        cost_estimate=pl.CostEstimate(flops=0, bytes_accessed=2 * MIB, transcendentals=0),
    )(at, *parts)


def project_kernel(count, temp_ref, *refs):
    blocks, (wq_ref, wkv_ref, q_ref, kv_ref) = refs[:count], refs[count:]
    head_dim = wq_ref.shape[1]
    x = jnp.concatenate([block[...] for block in blocks], axis=0)
    q = jnp.dot(x, wq_ref[...], preferred_element_type=jnp.float32)
    kv = jnp.dot(x, wkv_ref[...], preferred_element_type=jnp.float32)
    k = kv[:, :head_dim]
    q_scale = lax.rsqrt(jnp.mean(q * q, axis=-1, keepdims=True) + 1e-06)
    q_ref[...] = (q * q_scale * temp_ref[0, 0] / head_dim).astype(jnp.bfloat16)
    k_scale = lax.rsqrt(jnp.mean(k * k, axis=-1, keepdims=True) + 1e-06)
    kv_ref[:, :head_dim] = (k * k_scale).astype(jnp.bfloat16)
    kv_ref[:, head_dim:] = kv[:, head_dim:].astype(jnp.bfloat16)


def projected(blocks, wq, wkv, temp):
    rows = sum(b.shape[0] for b in blocks)
    vmem = pl.BlockSpec(memory_space=pltpu.VMEM)
    return pl.pallas_call(
        functools.partial(project_kernel, len(blocks)),
        in_specs=[pl.BlockSpec(memory_space=pltpu.SMEM)] + [vmem] * (len(blocks) + 2),
        out_specs=[vmem, vmem],
        out_shape=[
            jax.ShapeDtypeStruct((rows, wq.shape[1]), jnp.bfloat16),
            jax.ShapeDtypeStruct((rows, wkv.shape[1]), jnp.bfloat16),
        ],
        compiler_params=params(32),
        cost_estimate=pl.CostEstimate(
            flops=2 * rows * 2048 * 384, bytes_accessed=rows * 5632 + 1572864, transcendentals=0
        ),
    )(temp, *blocks, wq, wkv)


def masked_scores(q, keys, places, qpos, qspan, s_all, column, peak):
    s = lax.dot_general(q, keys, (((1,), (1,)), ((), ())), preferred_element_type=jnp.float32)
    for u, place in enumerate(places):
        lanes = slice(u * 128, (u + 1) * 128)
        part = jnp.where(qpos - place <= qspan, s[:, lanes], -1e30)
        s_all[:, column + u * 128 : column + (u + 1) * 128] = part
        peak = jnp.maximum(peak, part)
    return peak


def mixing(s_all, column, values, top, total, mixed):
    parts = []
    for u in range(values.shape[0] // 128):
        w = jnp.exp(s_all[:, column + u * 128 : column + (u + 1) * 128] - top)
        total = total + w
        parts.append(w.astype(jnp.bfloat16))
    w = jnp.concatenate(parts, axis=1)
    return total, mixed + jnp.dot(w, values, preferred_element_type=jnp.float32)


TILE = 256


def tile_of(t, at_ref, qpos_ref, qspan_ref):
    qpos, qspan = [], []
    for i in range(TILE // 128):
        placed = pl.ds(pl.multiple_of(at_ref[0, t * (TILE // 128) + i] * 128, 128), 128)
        qpos.append(jnp.broadcast_to(qpos_ref[placed, :], (128, 128)))
        qspan.append(jnp.broadcast_to(qspan_ref[placed, :], (128, 128)))
    rows = pl.ds(pl.multiple_of(t * TILE, TILE), TILE)
    return rows, jnp.concatenate(qpos, axis=0), jnp.concatenate(qspan, axis=0)


def attend_kernel(at_ref, qa, qb, *refs):
    parts, (qpos_ref, qspan_ref, kpos_ref, o_ref, q_all, k_all, v_all, s_all) = refs[:8], refs[8:]
    early, late = qa.shape[0], qb.shape[0]
    own_rows, head_dim = q_all.shape
    q_all[pl.ds(0, early), :] = qa[...]
    q_all[pl.ds(early, late), :] = qb[...]
    for i in range(4):
        for part, rows in (
            (parts[i], pl.ds(i * own_rows, early)),
            (parts[4 + i], pl.ds(i * own_rows + early, late)),
        ):
            k_all[rows, :] = part[:, :head_dim]
            v_all[rows, :] = part[:, head_dim:]
    offsets, wide = EARLY + LATE, 512
    cuts = [slice(start, start + wide) for start in range(0, k_all.shape[0], wide)]

    def one_tile(t, _):
        rows, qpos, qspan = tile_of(t, at_ref, qpos_ref, qspan_ref)
        q = q_all[rows, :]
        peak = jnp.full((TILE, 128), -1e30, jnp.float32)
        for cut in cuts:
            places = []
            for start in range(cut.start, cut.stop, 128):
                o = offsets[start % own_rows // 128]
                origin = start // own_rows
                places.append(kpos_ref[origin : origin + 1, o * 128 : (o + 1) * 128])
            peak = masked_scores(q, k_all[cut, :], places, qpos, qspan, s_all, cut.start, peak)
        top = jnp.broadcast_to(jnp.max(peak, axis=-1, keepdims=True), peak.shape)
        total = jnp.zeros((TILE, 128), jnp.float32)
        mixed = jnp.zeros((TILE, head_dim), jnp.float32)
        for cut in cuts:
            total, mixed = mixing(s_all, cut.start, v_all[cut, :], top, total, mixed)
        result = (mixed / jnp.sum(total, axis=-1, keepdims=True)).astype(jnp.bfloat16)
        for i in range(TILE // 128):
            placed = pl.ds(pl.multiple_of(at_ref[1, t * (TILE // 128) + i] * 128, 128), 128)
            o_ref[placed, :] = result[i * 128 : (i + 1) * 128, :]
        return 0

    lax.fori_loop(0, own_rows // TILE, one_tile, 0)


def attended(at, queries, keyvals, qpos, qspan, kpos):
    rows, head_dim = sum(q.shape[0] for q in queries), queries[0].shape[1]
    keys = sum(k.shape[0] for k in keyvals)
    vmem = pl.BlockSpec(memory_space=pltpu.VMEM)
    return pl.pallas_call(
        attend_kernel,
        in_specs=[pl.BlockSpec(memory_space=pltpu.SMEM)] + [vmem] * 13,
        out_specs=vmem,
        out_shape=jax.ShapeDtypeStruct((rows, head_dim), jnp.bfloat16),
        scratch_shapes=[
            pltpu.VMEM((rows, head_dim), jnp.bfloat16),
            pltpu.VMEM((keys, head_dim), jnp.bfloat16),
            pltpu.VMEM((keys, head_dim), jnp.bfloat16),
            pltpu.VMEM((TILE, keys), jnp.float32),
        ],
        compiler_params=params(24),
        cost_estimate=pl.CostEstimate(
            flops=40 * rows * keys * head_dim, bytes_accessed=4 * keys * head_dim, transcendentals=rows * keys
        ),
    )(at, *queries, *keyvals, qpos, qspan, kpos)


def output_kernel(m_ref, w_ref, x_ref, o_ref):
    mixed = jnp.concatenate([m_ref[h] for h in range(m_ref.shape[0])], axis=1)
    wide = 512
    for t in range(w_ref.shape[1] // wide):
        lanes = slice(t * wide, (t + 1) * wide)
        added = jnp.dot(mixed, w_ref[:, lanes], preferred_element_type=jnp.float32)
        o_ref[:, lanes] = (x_ref[:, lanes].astype(jnp.float32) + added).astype(jnp.bfloat16)


def outputs(mixed, w_out, x):
    return pl.pallas_call(
        output_kernel,
        out_shape=jax.ShapeDtypeStruct(x.shape, jnp.bfloat16),
        compiler_params=params(24),
        cost_estimate=pl.CostEstimate(
            flops=2 * 128 * 1024 * 2048, bytes_accessed=6 * MIB, transcendentals=0
        ),
    )(mixed, w_out, x)


def per_device(acts, order, doc_ids, gain, w_query, w_keyval, w_out, head_temp):
    inputs = acts[0]
    width = w_query.shape[2]
    heads = head_temp.shape[1]
    head_dim = width // heads
    yh, z, c = (lax.axis_index(a).astype(jnp.int32) for a in ("yh", "z", "c"))

    upper, lower, by_head = entry(inputs, gain, w_keyval[0], heads)

    blocks = {(0, 0): upper, (0, 1): lower}
    for distance in (1, 2, 3):
        for part in (0, 1):
            blocks[-distance, part] = shifted(blocks[1 - distance, part], "z", 1)
            blocks[distance, part] = shifted(blocks[distance - 1, part], "z", -1)
    blocks[4, 0] = shifted(blocks[-3, 0], "z", 1)
    blocks[4, 1] = shifted(blocks[3, 1], "z", -1)

    def rows_of(offset):
        at_offset = offset if offset <= 4 else offset - ZS
        return [blocks[at_offset, 0], blocks[at_offset, 1]]

    own_w = lax.all_to_all(by_head, "z", 0, 0, tiled=True)
    other_w = shifted(own_w, "yh", 1)
    wkv = assembled(jnp.stack([yh, c]), own_w, shifted(own_w, "c", 1), other_w, shifted(other_w, "c", 1))
    wq = lax.dynamic_slice_in_dim(w_query[0], z * head_dim, head_dim, axis=1)
    temp = lax.dynamic_slice_in_dim(head_temp, z, 1, axis=1)

    grid = order.reshape(2, ZS, 2, -1)
    grid = lax.dynamic_slice_in_dim(jnp.concatenate([grid, grid], axis=1), z, ZS, axis=1)
    grid = jnp.where(yh == 0, grid, grid[::-1])
    grid = jnp.where(c == 0, grid, grid[:, :, ::-1])
    kpos = grid.transpose(0, 2, 1, 3).reshape(4, -1)
    begins = jnp.sum(
        (doc_ids[None, :] < jnp.arange(1, 8, dtype=jnp.int32)[:, None]).astype(jnp.int32), axis=1
    )
    own_pos = kpos[0].reshape(-1, 1)
    began = jnp.max(jnp.where(begins[None, :] <= own_pos, begins[None, :], 0), axis=1, keepdims=True)
    lowest = jnp.int32(-(2**31))
    qspan = own_pos - began + lowest
    qpos = own_pos + lowest

    q_early, kv_early = projected(sum([rows_of(o) for o in EARLY], []), wq, wkv, temp)
    q_late, kv_late = projected(sum([rows_of(o) for o in LATE], []), wq, wkv, temp)
    over_early = shifted(kv_early, "yh", 1)
    _, over_later = lax.optimization_barrier((kv_late, over_early))
    over_late = shifted(kv_late, "yh", 1)
    keyvals = [kv_early, shifted(kv_early, "c", 1), over_early, shifted(over_later, "c", 1)]
    keyvals += [kv_late, shifted(kv_late, "c", 1), over_late, shifted(over_late, "c", 1)]
    offsets = jnp.array(EARLY + LATE, jnp.int32)
    at = jnp.stack([offsets, lax.rem(z + offsets, ZS)])
    mixed = attended(at, [q_early, q_late], keyvals, qpos, qspan, kpos)

    mixed = lax.all_to_all(mixed.reshape(ZS, -1, head_dim), "z", 0, 0, tiled=True)
    produced = outputs(mixed, w_out[0], inputs)
    handed = passed_along(produced, ("yl", "x"), 1)
    return (produced[None], handed[None])


def solution(mesh):
    devices = np.asarray(mesh.devices).reshape(2, ZS, 2, 2, 4)
    fine = Mesh(devices, ("yh", "z", "c", "yl", "x"))
    phase, blk = ("yl", "x"), ("yh", "z", "c")
    return jax.shard_map(
        per_device,
        mesh=fine,
        in_specs=(
            P(phase, blk, None),
            P(),
            P(),
            P(phase, None),
            P(phase, None, None),
            P(phase, blk, None),
            P(phase, None, None),
            P(phase, None),
        ),
        out_specs=(P(phase, blk, None), P(phase, blk, None)),
        check_vma=False,
    )
```

```python
import functools

import jax
import jax.numpy as jnp
import numpy as np
from jax import lax
from jax.experimental import pallas as pl
from jax.experimental.pallas import tpu as pltpu
from jax.sharding import Mesh
from jax.sharding import PartitionSpec as P

ZS = 8
EARLY, LATE = (0, 1, 7, 2, 6), (3, 5, 4)
MIB = 1024 * 1024


def shifted(block, axis, distance):
    count = lax.axis_size(axis)
    return lax.ppermute(block, axis, [(i, (i + distance) % count) for i in range(count)])


def passed_along(block, axis, distance):
    devices = range(lax.axis_size(axis))
    route = [(i - distance, i) for i in devices if i - distance in devices]
    return lax.ppermute(block, axis, route)


def params(mib):
    return pltpu.CompilerParams(vmem_limit_bytes=mib * MIB)


def entry_kernel(x_any, g_any, w_any, upper_ref, lower_ref, p_ref, x_ref, g_ref, w_ref, sems):
    copies = [
        pltpu.make_async_copy(source, target, sems.at[i])
        for i, (source, target) in enumerate(((x_any, x_ref), (g_any, g_ref), (w_any, w_ref)))
    ]
    for copy in copies:
        copy.start()
    copies[0].wait()
    copies[1].wait()
    half = upper_ref.shape[0]
    for part, n_ref in enumerate((upper_ref, lower_ref)):
        x = x_ref[part * half : (part + 1) * half, :].astype(jnp.float32)
        n_ref[...] = (
            x * lax.rsqrt(jnp.mean(x * x, axis=-1, keepdims=True) + 1e-05) * g_ref[...]
        ).astype(jnp.bfloat16)
    copies[2].wait()
    heads, _, wide = p_ref.shape
    width, head_dim = heads * wide // 2, wide // 2
    for h in range(heads):
        p_ref[h, :, :head_dim] = w_ref[:, h * head_dim : (h + 1) * head_dim]
        p_ref[h, :, head_dim:] = w_ref[:, width + h * head_dim : width + (h + 1) * head_dim]


def entry(x, gain, slab, heads):
    rows, columns = slab.shape
    vmem = pl.BlockSpec(memory_space=pltpu.VMEM)
    return pl.pallas_call(
        entry_kernel,
        in_specs=[pl.BlockSpec(memory_space=pltpu.HBM)] * 3,
        out_specs=[vmem] * 3,
        out_shape=[
            *[jax.ShapeDtypeStruct((x.shape[0] // 2, x.shape[1]), jnp.bfloat16)] * 2,
            jax.ShapeDtypeStruct((heads, rows, columns // heads), jnp.bfloat16),
        ],
        scratch_shapes=[
            pltpu.VMEM(x.shape, x.dtype),
            pltpu.VMEM(gain.shape, gain.dtype),
            pltpu.VMEM(slab.shape, slab.dtype),
            pltpu.SemaphoreType.DMA((3,)),
        ],
        compiler_params=params(54),
        cost_estimate=pl.CostEstimate(flops=0, bytes_accessed=3 * x.size * 2, transcendentals=0),
    )(x, gain, slab)


def assemble_kernel(at_ref, own, across, over, both, w_ref):
    rings, rows, _ = own.shape
    yh, core = at_ref[0], at_ref[1]
    for place, part in enumerate((own, across, over, both)):
        half, side = yh ^ (place // 2), core ^ (place % 2)
        for z in range(rings):
            start = half * (2 * rings * rows) + side * rows + z * 2 * rows
            w_ref[pl.ds(pl.multiple_of(start, rows), rows), :] = part[z]


def assembled(at, *parts):
    rings, rows, columns = parts[0].shape
    vmem = pl.BlockSpec(memory_space=pltpu.VMEM)
    return pl.pallas_call(
        assemble_kernel,
        in_specs=[pl.BlockSpec(memory_space=pltpu.SMEM)] + [vmem] * 4,
        out_specs=vmem,
        out_shape=jax.ShapeDtypeStruct((4 * rings * rows, columns), jnp.bfloat16),
        compiler_params=params(16),
        cost_estimate=pl.CostEstimate(flops=0, bytes_accessed=2 * MIB, transcendentals=0),
    )(at, *parts)


def project_kernel(count, temp_ref, *refs):
    blocks, (wq_ref, wkv_ref, q_ref, kv_ref) = refs[:count], refs[count:]
    head_dim = wq_ref.shape[1]
    x = jnp.concatenate([block[...] for block in blocks], axis=0)
    q = jnp.dot(x, wq_ref[...], preferred_element_type=jnp.float32)
    kv = jnp.dot(x, wkv_ref[...], preferred_element_type=jnp.float32)
    k = kv[:, :head_dim]
    q_scale = lax.rsqrt(jnp.mean(q * q, axis=-1, keepdims=True) + 1e-06)
    q_ref[...] = (q * q_scale * temp_ref[0, 0] / head_dim).astype(jnp.bfloat16)
    k_scale = lax.rsqrt(jnp.mean(k * k, axis=-1, keepdims=True) + 1e-06)
    kv_ref[:, :head_dim] = (k * k_scale).astype(jnp.bfloat16)
    kv_ref[:, head_dim:] = kv[:, head_dim:].astype(jnp.bfloat16)


def projected(blocks, wq, wkv, temp):
    rows = sum(b.shape[0] for b in blocks)
    vmem = pl.BlockSpec(memory_space=pltpu.VMEM)
    return pl.pallas_call(
        functools.partial(project_kernel, len(blocks)),
        in_specs=[pl.BlockSpec(memory_space=pltpu.SMEM)] + [vmem] * (len(blocks) + 2),
        out_specs=[vmem, vmem],
        out_shape=[
            jax.ShapeDtypeStruct((rows, wq.shape[1]), jnp.bfloat16),
            jax.ShapeDtypeStruct((rows, wkv.shape[1]), jnp.bfloat16),
        ],
        compiler_params=params(32),
        cost_estimate=pl.CostEstimate(
            flops=2 * rows * 2048 * 384, bytes_accessed=rows * 5632 + 1572864, transcendentals=0
        ),
    )(temp, *blocks, wq, wkv)


def masked_scores(q, keys, places, qpos, qspan, s_all, column, peak):
    s = lax.dot_general(q, keys, (((1,), (1,)), ((), ())), preferred_element_type=jnp.float32)
    for u, place in enumerate(places):
        lanes = slice(u * 128, (u + 1) * 128)
        part = jnp.where(qpos - place <= qspan, s[:, lanes], -1e30)
        s_all[:, column + u * 128 : column + (u + 1) * 128] = part
        peak = jnp.maximum(peak, part)
    return peak


def mixing(s_all, column, values, top, total, mixed):
    parts = []
    for u in range(values.shape[0] // 128):
        w = jnp.exp(s_all[:, column + u * 128 : column + (u + 1) * 128] - top)
        total = total + w
        parts.append(w.astype(jnp.bfloat16))
    w = jnp.concatenate(parts, axis=1)
    return total, mixed + jnp.dot(w, values, preferred_element_type=jnp.float32)


TILE = 256


def tile_of(t, at_ref, qpos_ref, qspan_ref):
    qpos, qspan = [], []
    for i in range(TILE // 128):
        placed = pl.ds(pl.multiple_of(at_ref[0, t * (TILE // 128) + i] * 128, 128), 128)
        qpos.append(jnp.broadcast_to(qpos_ref[placed, :], (128, 128)))
        qspan.append(jnp.broadcast_to(qspan_ref[placed, :], (128, 128)))
    rows = pl.ds(pl.multiple_of(t * TILE, TILE), TILE)
    return rows, jnp.concatenate(qpos, axis=0), jnp.concatenate(qspan, axis=0)


def attend_kernel(at_ref, qa, qb, *refs):
    parts, (qpos_ref, qspan_ref, kpos_ref, o_ref, q_all, k_all, v_all, s_all) = refs[:8], refs[8:]
    early, late = qa.shape[0], qb.shape[0]
    own_rows, head_dim = q_all.shape
    q_all[pl.ds(0, early), :] = qa[...]
    q_all[pl.ds(early, late), :] = qb[...]
    for i in range(4):
        for part, rows in (
            (parts[i], pl.ds(i * own_rows, early)),
            (parts[4 + i], pl.ds(i * own_rows + early, late)),
        ):
            k_all[rows, :] = part[:, :head_dim]
            v_all[rows, :] = part[:, head_dim:]
    offsets, wide = EARLY + LATE, 512
    cuts = [slice(start, start + wide) for start in range(0, k_all.shape[0], wide)]

    def one_tile(t, _):
        rows, qpos, qspan = tile_of(t, at_ref, qpos_ref, qspan_ref)
        q = q_all[rows, :]
        peak = jnp.full((TILE, 128), -1e30, jnp.float32)
        for cut in cuts:
            places = []
            for start in range(cut.start, cut.stop, 128):
                o = offsets[start % own_rows // 128]
                origin = start // own_rows
                places.append(kpos_ref[origin : origin + 1, o * 128 : (o + 1) * 128])
            peak = masked_scores(q, k_all[cut, :], places, qpos, qspan, s_all, cut.start, peak)
        top = jnp.broadcast_to(jnp.max(peak, axis=-1, keepdims=True), peak.shape)
        total = jnp.zeros((TILE, 128), jnp.float32)
        mixed = jnp.zeros((TILE, head_dim), jnp.float32)
        for cut in cuts:
            total, mixed = mixing(s_all, cut.start, v_all[cut, :], top, total, mixed)
        result = (mixed / jnp.sum(total, axis=-1, keepdims=True)).astype(jnp.bfloat16)
        for i in range(TILE // 128):
            placed = pl.ds(pl.multiple_of(at_ref[1, t * (TILE // 128) + i] * 128, 128), 128)
            o_ref[placed, :] = result[i * 128 : (i + 1) * 128, :]
        return 0

    lax.fori_loop(0, own_rows // TILE, one_tile, 0)


def attended(at, queries, keyvals, qpos, qspan, kpos):
    rows, head_dim = sum(q.shape[0] for q in queries), queries[0].shape[1]
    keys = sum(k.shape[0] for k in keyvals)
    vmem = pl.BlockSpec(memory_space=pltpu.VMEM)
    return pl.pallas_call(
        attend_kernel,
        in_specs=[pl.BlockSpec(memory_space=pltpu.SMEM)] + [vmem] * 13,
        out_specs=vmem,
        out_shape=jax.ShapeDtypeStruct((rows, head_dim), jnp.bfloat16),
        scratch_shapes=[
            pltpu.VMEM((rows, head_dim), jnp.bfloat16),
            pltpu.VMEM((keys, head_dim), jnp.bfloat16),
            pltpu.VMEM((keys, head_dim), jnp.bfloat16),
            pltpu.VMEM((TILE, keys), jnp.float32),
        ],
        compiler_params=params(24),
        cost_estimate=pl.CostEstimate(
            flops=40 * rows * keys * head_dim, bytes_accessed=4 * keys * head_dim, transcendentals=rows * keys
        ),
    )(at, *queries, *keyvals, qpos, qspan, kpos)


def output_kernel(m_ref, w_ref, x_ref, o_ref):
    mixed = jnp.concatenate([m_ref[h] for h in range(m_ref.shape[0])], axis=1)
    wide = 512
    for t in range(w_ref.shape[1] // wide):
        lanes = slice(t * wide, (t + 1) * wide)
        added = jnp.dot(mixed, w_ref[:, lanes], preferred_element_type=jnp.float32)
        o_ref[:, lanes] = (x_ref[:, lanes].astype(jnp.float32) + added).astype(jnp.bfloat16)


def outputs(mixed, w_out, x):
    return pl.pallas_call(
        output_kernel,
        out_shape=jax.ShapeDtypeStruct(x.shape, jnp.bfloat16),
        compiler_params=params(24),
        cost_estimate=pl.CostEstimate(
            flops=2 * 128 * 1024 * 2048, bytes_accessed=6 * MIB, transcendentals=0
        ),
    )(mixed, w_out, x)


def per_device(acts, order, doc_ids, gain, w_query, w_keyval, w_out, head_temp):
    inputs = acts[0]
    width = w_query.shape[2]
    heads = head_temp.shape[1]
    head_dim = width // heads
    yh, z, c = (lax.axis_index(a).astype(jnp.int32) for a in ("yh", "z", "c"))

    upper, lower, by_head = entry(inputs, gain, w_keyval[0], heads)

    blocks = {(0, 0): upper, (0, 1): lower}
    for distance in (1, 2, 3):
        for part in (0, 1):
            blocks[-distance, part] = shifted(blocks[1 - distance, part], "z", 1)
            blocks[distance, part] = shifted(blocks[distance - 1, part], "z", -1)
    blocks[4, 0] = shifted(blocks[-3, 0], "z", 1)
    blocks[4, 1] = shifted(blocks[3, 1], "z", -1)

    def rows_of(offset):
        at_offset = offset if offset <= 4 else offset - ZS
        return [blocks[at_offset, 0], blocks[at_offset, 1]]

    own_w = lax.all_to_all(by_head, "z", 0, 0, tiled=True)
    other_w = shifted(own_w, "yh", 1)
    wkv = assembled(jnp.stack([yh, c]), own_w, shifted(own_w, "c", 1), other_w, shifted(other_w, "c", 1))
    wq = lax.dynamic_slice_in_dim(w_query[0], z * head_dim, head_dim, axis=1)
    temp = lax.dynamic_slice_in_dim(head_temp, z, 1, axis=1)

    grid = order.reshape(2, ZS, 2, -1)
    grid = lax.dynamic_slice_in_dim(jnp.concatenate([grid, grid], axis=1), z, ZS, axis=1)
    grid = jnp.where(yh == 0, grid, grid[::-1])
    grid = jnp.where(c == 0, grid, grid[:, :, ::-1])
    kpos = grid.transpose(0, 2, 1, 3).reshape(4, -1)
    begins = jnp.sum(
        (doc_ids[None, :] < jnp.arange(1, 8, dtype=jnp.int32)[:, None]).astype(jnp.int32), axis=1
    )
    own_pos = kpos[0].reshape(-1, 1)
    began = jnp.max(jnp.where(begins[None, :] <= own_pos, begins[None, :], 0), axis=1, keepdims=True)
    lowest = jnp.int32(-(2**31))
    qspan = own_pos - began + lowest
    qpos = own_pos + lowest

    q_early, kv_early = projected(sum([rows_of(o) for o in EARLY], []), wq, wkv, temp)
    q_late, kv_late = projected(sum([rows_of(o) for o in LATE], []), wq, wkv, temp)
    over_early = shifted(kv_early, "yh", 1)
    _, over_later = lax.optimization_barrier((kv_late, over_early))
    over_late = shifted(kv_late, "yh", 1)
    keyvals = [kv_early, shifted(kv_early, "c", 1), over_early, shifted(over_later, "c", 1)]
    keyvals += [kv_late, shifted(kv_late, "c", 1), over_late, shifted(over_late, "c", 1)]
    offsets = jnp.array(EARLY + LATE, jnp.int32)
    at = jnp.stack([offsets, lax.rem(z + offsets, ZS)])
    mixed = attended(at, [q_early, q_late], keyvals, qpos, qspan, kpos)

    mixed = lax.all_to_all(mixed.reshape(ZS, -1, head_dim), "z", 0, 0, tiled=True)
    produced = outputs(mixed, w_out[0], inputs)
    handed = passed_along(produced, ("yl", "x"), 1)
    return (produced[None], handed[None])


def solution(mesh):
    devices = np.asarray(mesh.devices).reshape(2, ZS, 2, 2, 4)
    fine = Mesh(devices, ("yh", "z", "c", "yl", "x"))
    phase, blk = ("yl", "x"), ("yh", "z", "c")
    return jax.shard_map(
        per_device,
        mesh=fine,
        in_specs=(
            P(phase, blk, None),
            P(),
            P(),
            P(phase, None),
            P(phase, None, None),
            P(phase, blk, None),
            P(phase, None, None),
            P(phase, None),
        ),
        out_specs=(P(phase, blk, None), P(phase, blk, None)),
        check_vma=False,
    )
```

```python
import functools

import jax
import jax.numpy as jnp
import numpy as np
from jax import lax
from jax.experimental import pallas as pl
from jax.experimental.pallas import tpu as pltpu
from jax.sharding import Mesh
from jax.sharding import PartitionSpec as P

ZS = 8
EARLY, LATE = (0, 1, 7, 2, 6), (3, 5, 4)
MIB = 1024 * 1024


def shifted(block, axis, distance):
    count = lax.axis_size(axis)
    return lax.ppermute(block, axis, [(i, (i + distance) % count) for i in range(count)])


def passed_along(block, axis, distance):
    devices = range(lax.axis_size(axis))
    route = [(i - distance, i) for i in devices if i - distance in devices]
    return lax.ppermute(block, axis, route)


def params(mib):
    return pltpu.CompilerParams(vmem_limit_bytes=mib * MIB)


def entry_kernel(x_any, g_any, w_any, upper_ref, lower_ref, p_ref, x_ref, g_ref, w_ref, sems):
    copies = [
        pltpu.make_async_copy(source, target, sems.at[i])
        for i, (source, target) in enumerate(((x_any, x_ref), (g_any, g_ref), (w_any, w_ref)))
    ]
    for copy in copies:
        copy.start()
    copies[0].wait()
    copies[1].wait()
    half = upper_ref.shape[0]
    for part, n_ref in enumerate((upper_ref, lower_ref)):
        x = x_ref[part * half : (part + 1) * half, :].astype(jnp.float32)
        n_ref[...] = (
            x * lax.rsqrt(jnp.mean(x * x, axis=-1, keepdims=True) + 1e-05) * g_ref[...]
        ).astype(jnp.bfloat16)
    copies[2].wait()
    heads, _, wide = p_ref.shape
    width, head_dim = heads * wide // 2, wide // 2
    for h in range(heads):
        p_ref[h, :, :head_dim] = w_ref[:, h * head_dim : (h + 1) * head_dim]
        p_ref[h, :, head_dim:] = w_ref[:, width + h * head_dim : width + (h + 1) * head_dim]


def entry(x, gain, slab, heads):
    rows, columns = slab.shape
    vmem = pl.BlockSpec(memory_space=pltpu.VMEM)
    return pl.pallas_call(
        entry_kernel,
        in_specs=[pl.BlockSpec(memory_space=pltpu.HBM)] * 3,
        out_specs=[vmem] * 3,
        out_shape=[
            *[jax.ShapeDtypeStruct((x.shape[0] // 2, x.shape[1]), jnp.bfloat16)] * 2,
            jax.ShapeDtypeStruct((heads, rows, columns // heads), jnp.bfloat16),
        ],
        scratch_shapes=[
            pltpu.VMEM(x.shape, x.dtype),
            pltpu.VMEM(gain.shape, gain.dtype),
            pltpu.VMEM(slab.shape, slab.dtype),
            pltpu.SemaphoreType.DMA((3,)),
        ],
        compiler_params=params(54),
        cost_estimate=pl.CostEstimate(flops=0, bytes_accessed=3 * x.size * 2, transcendentals=0),
    )(x, gain, slab)


def assemble_kernel(at_ref, own, across, over, both, w_ref):
    rings, rows, _ = own.shape
    yh, core = at_ref[0], at_ref[1]
    for place, part in enumerate((own, across, over, both)):
        half, side = yh ^ (place // 2), core ^ (place % 2)
        for z in range(rings):
            start = half * (2 * rings * rows) + side * rows + z * 2 * rows
            w_ref[pl.ds(pl.multiple_of(start, rows), rows), :] = part[z]


def assembled(at, *parts):
    rings, rows, columns = parts[0].shape
    vmem = pl.BlockSpec(memory_space=pltpu.VMEM)
    return pl.pallas_call(
        assemble_kernel,
        in_specs=[pl.BlockSpec(memory_space=pltpu.SMEM)] + [vmem] * 4,
        out_specs=vmem,
        out_shape=jax.ShapeDtypeStruct((4 * rings * rows, columns), jnp.bfloat16),
        compiler_params=params(16),
        cost_estimate=pl.CostEstimate(flops=0, bytes_accessed=2 * MIB, transcendentals=0),
    )(at, *parts)


def project_kernel(count, temp_ref, *refs):
    blocks, (wq_ref, wkv_ref, q_ref, kv_ref) = refs[:count], refs[count:]
    head_dim = wq_ref.shape[1]
    x = jnp.concatenate([block[...] for block in blocks], axis=0)
    q = jnp.dot(x, wq_ref[...], preferred_element_type=jnp.float32)
    kv = jnp.dot(x, wkv_ref[...], preferred_element_type=jnp.float32)
    k = kv[:, :head_dim]
    q_scale = lax.rsqrt(jnp.mean(q * q, axis=-1, keepdims=True) + 1e-06)
    q_ref[...] = (q * q_scale * temp_ref[0, 0] / head_dim).astype(jnp.bfloat16)
    k_scale = lax.rsqrt(jnp.mean(k * k, axis=-1, keepdims=True) + 1e-06)
    kv_ref[:, :head_dim] = (k * k_scale).astype(jnp.bfloat16)
    kv_ref[:, head_dim:] = kv[:, head_dim:].astype(jnp.bfloat16)


def projected(blocks, wq, wkv, temp):
    rows = sum(b.shape[0] for b in blocks)
    vmem = pl.BlockSpec(memory_space=pltpu.VMEM)
    return pl.pallas_call(
        functools.partial(project_kernel, len(blocks)),
        in_specs=[pl.BlockSpec(memory_space=pltpu.SMEM)] + [vmem] * (len(blocks) + 2),
        out_specs=[vmem, vmem],
        out_shape=[
            jax.ShapeDtypeStruct((rows, wq.shape[1]), jnp.bfloat16),
            jax.ShapeDtypeStruct((rows, wkv.shape[1]), jnp.bfloat16),
        ],
        compiler_params=params(32),
        cost_estimate=pl.CostEstimate(
            flops=2 * rows * 2048 * 384, bytes_accessed=rows * 5632 + 1572864, transcendentals=0
        ),
    )(temp, *blocks, wq, wkv)


def masked_scores(q, keys, places, qpos, qspan, s_all, column, peak):
    s = lax.dot_general(q, keys, (((1,), (1,)), ((), ())), preferred_element_type=jnp.float32)
    for u, place in enumerate(places):
        lanes = slice(u * 128, (u + 1) * 128)
        part = jnp.where(qpos - place <= qspan, s[:, lanes], -1e30)
        s_all[:, column + u * 128 : column + (u + 1) * 128] = part
        peak = jnp.maximum(peak, part)
    return peak


def mixing(s_all, column, values, top, total, mixed):
    parts = []
    for u in range(values.shape[0] // 128):
        w = jnp.exp(s_all[:, column + u * 128 : column + (u + 1) * 128] - top)
        total = total + w
        parts.append(w.astype(jnp.bfloat16))
    w = jnp.concatenate(parts, axis=1)
    return total, mixed + jnp.dot(w, values, preferred_element_type=jnp.float32)


TILE = 256


def tile_of(t, at_ref, qpos_ref, qspan_ref):
    qpos, qspan = [], []
    for i in range(TILE // 128):
        placed = pl.ds(pl.multiple_of(at_ref[0, t * (TILE // 128) + i] * 128, 128), 128)
        qpos.append(jnp.broadcast_to(qpos_ref[placed, :], (128, 128)))
        qspan.append(jnp.broadcast_to(qspan_ref[placed, :], (128, 128)))
    rows = pl.ds(pl.multiple_of(t * TILE, TILE), TILE)
    return rows, jnp.concatenate(qpos, axis=0), jnp.concatenate(qspan, axis=0)


def laid_out(parts, k_all, v_all):
    head_dim, start = k_all.shape[1], 0
    for early, late in parts:
        for part in (early, late):
            rows = pl.ds(start, part.shape[0])
            k_all[rows, :] = part[:, :head_dim]
            v_all[rows, :] = part[:, head_dim:]
            start += part.shape[0]


def weighed(q, peak, first, kpos_ref, qpos, qspan, k_all, v_all, s_all):
    offsets, wide = EARLY + LATE, 512
    cuts = [slice(start, start + wide) for start in range(0, k_all.shape[0], wide)]
    for cut in cuts:
        places = []
        for start in range(cut.start, cut.stop, 128):
            origin, block = divmod(start // 128, len(offsets))
            origin, o = origin + first, offsets[block]
            places.append(kpos_ref[origin : origin + 1, o * 128 : (o + 1) * 128])
        peak = masked_scores(q, k_all[cut, :], places, qpos, qspan, s_all, cut.start, peak)
    top = jnp.broadcast_to(jnp.max(peak, axis=-1, keepdims=True), peak.shape)
    total = jnp.zeros((TILE, 128), jnp.float32)
    mixed = jnp.zeros((TILE, q.shape[1]), jnp.float32)
    for cut in cuts:
        total, mixed = mixing(s_all, cut.start, v_all[cut, :], top, total, mixed)
    return top, total, mixed


def own_kernel(at_ref, qa, qb, early, late, qpos_ref, qspan_ref, kpos_ref, q_out, acc, top_out, total_out, k_all, v_all, s_all):
    q_out[pl.ds(0, qa.shape[0]), :] = qa[...]
    q_out[pl.ds(qa.shape[0], qb.shape[0]), :] = qb[...]
    laid_out([(early, late)], k_all, v_all)

    def one_tile(t, _):
        rows, qpos, qspan = tile_of(t, at_ref, qpos_ref, qspan_ref)
        peak = jnp.full((TILE, 128), -1e30, jnp.float32)
        top, total, mixed = weighed(q_out[rows, :], peak, 0, kpos_ref, qpos, qspan, k_all, v_all, s_all)
        acc[rows, :] = mixed
        total_out[rows, :] = total
        top_out[rows, :] = top
        return 0

    lax.fori_loop(0, q_out.shape[0] // TILE, one_tile, 0)


def others_kernel(at_ref, q_ref, acc, top_ref, total_ref, *refs):
    parts, (qpos_ref, qspan_ref, kpos_ref, o_ref, k_all, v_all, s_all) = refs[:6], refs[6:]
    laid_out(list(zip(parts[:3], parts[3:])), k_all, v_all)

    def one_tile(t, _):
        rows, qpos, qspan = tile_of(t, at_ref, qpos_ref, qspan_ref)
        before = top_ref[rows, :]
        top, total, mixed = weighed(
            q_ref[rows, :], before, 1, kpos_ref, qpos, qspan, k_all, v_all, s_all
        )
        kept = jnp.exp(before - top)
        weight = jnp.sum(total_ref[rows, :] * kept + total, axis=-1, keepdims=True)
        result = ((acc[rows, :] * kept + mixed) / weight).astype(jnp.bfloat16)
        for i in range(TILE // 128):
            placed = pl.ds(pl.multiple_of(at_ref[1, t * (TILE // 128) + i] * 128, 128), 128)
            o_ref[placed, :] = result[i * 128 : (i + 1) * 128, :]
        return 0

    lax.fori_loop(0, q_ref.shape[0] // TILE, one_tile, 0)


def attended(kernel, out_shape, keys, at, *operands):
    head_dim = 128
    rows = operands[0].shape[0]
    vmem = pl.BlockSpec(memory_space=pltpu.VMEM)
    return pl.pallas_call(
        kernel,
        in_specs=[pl.BlockSpec(memory_space=pltpu.SMEM)] + [vmem] * len(operands),
        out_specs=[vmem] * len(out_shape),
        out_shape=out_shape,
        scratch_shapes=[
            pltpu.VMEM((keys, head_dim), jnp.bfloat16),
            pltpu.VMEM((keys, head_dim), jnp.bfloat16),
            pltpu.VMEM((TILE, keys), jnp.float32),
        ],
        compiler_params=params(16),
        cost_estimate=pl.CostEstimate(
            flops=24 * rows * keys * head_dim, bytes_accessed=4 * keys * head_dim, transcendentals=rows * keys
        ),
    )(at, *operands)


def output_kernel(m_ref, w_ref, x_ref, o_ref):
    mixed = jnp.concatenate([m_ref[h] for h in range(m_ref.shape[0])], axis=1)
    wide = 512
    for t in range(w_ref.shape[1] // wide):
        lanes = slice(t * wide, (t + 1) * wide)
        added = jnp.dot(mixed, w_ref[:, lanes], preferred_element_type=jnp.float32)
        o_ref[:, lanes] = (x_ref[:, lanes].astype(jnp.float32) + added).astype(jnp.bfloat16)


def outputs(mixed, w_out, x):
    return pl.pallas_call(
        output_kernel,
        out_shape=jax.ShapeDtypeStruct(x.shape, jnp.bfloat16),
        compiler_params=params(24),
        cost_estimate=pl.CostEstimate(
            flops=2 * 128 * 1024 * 2048, bytes_accessed=6 * MIB, transcendentals=0
        ),
    )(mixed, w_out, x)


def per_device(acts, order, doc_ids, gain, w_query, w_keyval, w_out, head_temp):
    inputs = acts[0]
    width = w_query.shape[2]
    heads = head_temp.shape[1]
    head_dim = width // heads
    yh, z, c = (lax.axis_index(a).astype(jnp.int32) for a in ("yh", "z", "c"))

    upper, lower, by_head = entry(inputs, gain, w_keyval[0], heads)

    blocks = {(0, 0): upper, (0, 1): lower}
    for distance in (1, 2, 3):
        for part in (0, 1):
            blocks[-distance, part] = shifted(blocks[1 - distance, part], "z", 1)
            blocks[distance, part] = shifted(blocks[distance - 1, part], "z", -1)
    blocks[4, 0] = shifted(blocks[-3, 0], "z", 1)
    blocks[4, 1] = shifted(blocks[3, 1], "z", -1)

    def rows_of(offset):
        at_offset = offset if offset <= 4 else offset - ZS
        return [blocks[at_offset, 0], blocks[at_offset, 1]]

    own_w = lax.all_to_all(by_head, "z", 0, 0, tiled=True)
    other_w = shifted(own_w, "yh", 1)
    wkv = assembled(jnp.stack([yh, c]), own_w, shifted(own_w, "c", 1), other_w, shifted(other_w, "c", 1))
    wq = lax.dynamic_slice_in_dim(w_query[0], z * head_dim, head_dim, axis=1)
    temp = lax.dynamic_slice_in_dim(head_temp, z, 1, axis=1)

    grid = order.reshape(2, ZS, 2, -1)
    grid = lax.dynamic_slice_in_dim(jnp.concatenate([grid, grid], axis=1), z, ZS, axis=1)
    grid = jnp.where(yh == 0, grid, grid[::-1])
    grid = jnp.where(c == 0, grid, grid[:, :, ::-1])
    kpos = grid.transpose(0, 2, 1, 3).reshape(4, -1)
    begins = jnp.sum(
        (doc_ids[None, :] < jnp.arange(1, 8, dtype=jnp.int32)[:, None]).astype(jnp.int32), axis=1
    )
    own_pos = kpos[0].reshape(-1, 1)
    began = jnp.max(jnp.where(begins[None, :] <= own_pos, begins[None, :], 0), axis=1, keepdims=True)
    lowest = jnp.int32(-(2**31))
    qspan = own_pos - began + lowest
    qpos = own_pos + lowest

    q_early, kv_early = projected(sum([rows_of(o) for o in EARLY], []), wq, wkv, temp)
    q_late, kv_late = projected(sum([rows_of(o) for o in LATE], []), wq, wkv, temp)
    over_early = shifted(kv_early, "yh", 1)
    _, over_later = lax.optimization_barrier((kv_late, over_early))
    over_late = shifted(kv_late, "yh", 1)
    offsets = jnp.array(EARLY + LATE, jnp.int32)
    at = jnp.stack([offsets, lax.rem(z + offsets, ZS)])
    rows = q_early.shape[0] + q_late.shape[0]
    narrow = jax.ShapeDtypeStruct((rows, head_dim), jnp.bfloat16)
    wide = jax.ShapeDtypeStruct((rows, head_dim), jnp.float32)
    where = (qpos, qspan, kpos)
    state = attended(own_kernel, [narrow] + [wide] * 3, rows, at, q_early, q_late, kv_early, kv_late, *where)
    _, over_last = lax.optimization_barrier((state[0], over_late))
    others = [shifted(kv_early, "c", 1), over_early, shifted(over_later, "c", 1)]
    others += [shifted(kv_late, "c", 1), over_late, shifted(over_last, "c", 1)]
    (mixed,) = attended(others_kernel, [narrow], 3 * rows, at, *state, *others, *where)
    mixed = lax.all_to_all(mixed.reshape(ZS, -1, head_dim), "z", 0, 0, tiled=True)
    produced = outputs(mixed, w_out[0], inputs)
    handed = passed_along(produced, ("yl", "x"), 1)
    return (produced[None], handed[None])


def solution(mesh):
    devices = np.asarray(mesh.devices).reshape(2, ZS, 2, 2, 4)
    fine = Mesh(devices, ("yh", "z", "c", "yl", "x"))
    phase, blk = ("yl", "x"), ("yh", "z", "c")
    return jax.shard_map(
        per_device,
        mesh=fine,
        in_specs=(
            P(phase, blk, None),
            P(),
            P(),
            P(phase, None),
            P(phase, None, None),
            P(phase, blk, None),
            P(phase, None, None),
            P(phase, None),
        ),
        out_specs=(P(phase, blk, None), P(phase, blk, None)),
        check_vma=False,
    )
```

```python
import functools

import jax
import jax.numpy as jnp
import numpy as np
from jax import lax
from jax.experimental import pallas as pl
from jax.experimental.pallas import tpu as pltpu
from jax.sharding import Mesh
from jax.sharding import PartitionSpec as P

ZS = 8
EARLY, LATE = (0, 1, 7, 2, 6), (3, 5, 4)
MIB = 1024 * 1024


def shifted(block, axis, distance):
    count = lax.axis_size(axis)
    return lax.ppermute(block, axis, [(i, (i + distance) % count) for i in range(count)])


def passed_along(block, axis, distance):
    devices = range(lax.axis_size(axis))
    route = [(i - distance, i) for i in devices if i - distance in devices]
    return lax.ppermute(block, axis, route)


def params(mib):
    return pltpu.CompilerParams(vmem_limit_bytes=mib * MIB)


def entry_kernel(x_any, g_any, w_any, upper_ref, lower_ref, p_ref, x_ref, g_ref, w_ref, sems):
    copies = [
        pltpu.make_async_copy(source, target, sems.at[i])
        for i, (source, target) in enumerate(((x_any, x_ref), (g_any, g_ref), (w_any, w_ref)))
    ]
    for copy in copies:
        copy.start()
    copies[0].wait()
    copies[1].wait()
    half = upper_ref.shape[0]
    for part, n_ref in enumerate((upper_ref, lower_ref)):
        x = x_ref[part * half : (part + 1) * half, :].astype(jnp.float32)
        n_ref[...] = (
            x * lax.rsqrt(jnp.mean(x * x, axis=-1, keepdims=True) + 1e-05) * g_ref[...]
        ).astype(jnp.bfloat16)
    copies[2].wait()
    heads, _, wide = p_ref.shape
    width, head_dim = heads * wide // 2, wide // 2
    for h in range(heads):
        p_ref[h, :, :head_dim] = w_ref[:, h * head_dim : (h + 1) * head_dim]
        p_ref[h, :, head_dim:] = w_ref[:, width + h * head_dim : width + (h + 1) * head_dim]


def entry(x, gain, slab, heads):
    rows, columns = slab.shape
    vmem = pl.BlockSpec(memory_space=pltpu.VMEM)
    return pl.pallas_call(
        entry_kernel,
        in_specs=[pl.BlockSpec(memory_space=pltpu.HBM)] * 3,
        out_specs=[vmem] * 3,
        out_shape=[
            *[jax.ShapeDtypeStruct((x.shape[0] // 2, x.shape[1]), jnp.bfloat16)] * 2,
            jax.ShapeDtypeStruct((heads, rows, columns // heads), jnp.bfloat16),
        ],
        scratch_shapes=[
            pltpu.VMEM(x.shape, x.dtype),
            pltpu.VMEM(gain.shape, gain.dtype),
            pltpu.VMEM(slab.shape, slab.dtype),
            pltpu.SemaphoreType.DMA((3,)),
        ],
        compiler_params=params(54),
        cost_estimate=pl.CostEstimate(flops=0, bytes_accessed=3 * x.size * 2, transcendentals=0),
    )(x, gain, slab)


def assemble_kernel(at_ref, own, across, over, both, w_ref):
    rings, rows, _ = own.shape
    yh, core = at_ref[0], at_ref[1]
    for place, part in enumerate((own, across, over, both)):
        half, side = yh ^ (place // 2), core ^ (place % 2)
        for z in range(rings):
            start = half * (2 * rings * rows) + side * rows + z * 2 * rows
            w_ref[pl.ds(pl.multiple_of(start, rows), rows), :] = part[z]


def assembled(at, *parts):
    rings, rows, columns = parts[0].shape
    vmem = pl.BlockSpec(memory_space=pltpu.VMEM)
    return pl.pallas_call(
        assemble_kernel,
        in_specs=[pl.BlockSpec(memory_space=pltpu.SMEM)] + [vmem] * 4,
        out_specs=vmem,
        out_shape=jax.ShapeDtypeStruct((4 * rings * rows, columns), jnp.bfloat16),
        compiler_params=params(16),
        cost_estimate=pl.CostEstimate(flops=0, bytes_accessed=2 * MIB, transcendentals=0),
    )(at, *parts)


def project_kernel(count, temp_ref, *refs):
    blocks, (wq_ref, wkv_ref, q_ref, kv_ref) = refs[:count], refs[count:]
    head_dim = wq_ref.shape[1]
    x = jnp.concatenate([block[...] for block in blocks], axis=0)
    q = jnp.dot(x, wq_ref[...], preferred_element_type=jnp.float32)
    kv = jnp.dot(x, wkv_ref[...], preferred_element_type=jnp.float32)
    k = kv[:, :head_dim]
    q_scale = lax.rsqrt(jnp.mean(q * q, axis=-1, keepdims=True) + 1e-06)
    q_ref[...] = (q * q_scale * temp_ref[0, 0] / head_dim).astype(jnp.bfloat16)
    k_scale = lax.rsqrt(jnp.mean(k * k, axis=-1, keepdims=True) + 1e-06)
    kv_ref[:, :head_dim] = (k * k_scale).astype(jnp.bfloat16)
    kv_ref[:, head_dim:] = kv[:, head_dim:].astype(jnp.bfloat16)


def projected(blocks, wq, wkv, temp):
    rows = sum(b.shape[0] for b in blocks)
    vmem = pl.BlockSpec(memory_space=pltpu.VMEM)
    return pl.pallas_call(
        functools.partial(project_kernel, len(blocks)),
        in_specs=[pl.BlockSpec(memory_space=pltpu.SMEM)] + [vmem] * (len(blocks) + 2),
        out_specs=[vmem, vmem],
        out_shape=[
            jax.ShapeDtypeStruct((rows, wq.shape[1]), jnp.bfloat16),
            jax.ShapeDtypeStruct((rows, wkv.shape[1]), jnp.bfloat16),
        ],
        compiler_params=params(32),
        cost_estimate=pl.CostEstimate(
            flops=2 * rows * 2048 * 384, bytes_accessed=rows * 5632 + 1572864, transcendentals=0
        ),
    )(temp, *blocks, wq, wkv)


def masked_scores(q, keys, places, qpos, qspan, s_all, column, peak):
    s = lax.dot_general(q, keys, (((1,), (1,)), ((), ())), preferred_element_type=jnp.float32)
    for u, place in enumerate(places):
        lanes = slice(u * 128, (u + 1) * 128)
        part = jnp.where(qpos - place <= qspan, s[:, lanes], -1e30)
        s_all[:, column + u * 128 : column + (u + 1) * 128] = part
        peak = jnp.maximum(peak, part)
    return peak


def mixing(s_all, column, values, top, total, mixed):
    parts = []
    for u in range(values.shape[0] // 128):
        w = jnp.exp(s_all[:, column + u * 128 : column + (u + 1) * 128] - top)
        total = total + w
        parts.append(w.astype(jnp.bfloat16))
    w = jnp.concatenate(parts, axis=1)
    return total, mixed + jnp.dot(w, values, preferred_element_type=jnp.float32)


TILE = 256


def tile_of(t, at_ref, qpos_ref, qspan_ref):
    qpos, qspan = [], []
    for i in range(TILE // 128):
        placed = pl.ds(pl.multiple_of(at_ref[0, t * (TILE // 128) + i] * 128, 128), 128)
        qpos.append(jnp.broadcast_to(qpos_ref[placed, :], (128, 128)))
        qspan.append(jnp.broadcast_to(qspan_ref[placed, :], (128, 128)))
    rows = pl.ds(pl.multiple_of(t * TILE, TILE), TILE)
    return rows, jnp.concatenate(qpos, axis=0), jnp.concatenate(qspan, axis=0)


def attend_kernel(at_ref, qa, qb, *refs):
    parts, (qpos_ref, qspan_ref, kpos_ref, o_ref, q_all, k_all, v_all, s_all) = refs[:8], refs[8:]
    early, late = qa.shape[0], qb.shape[0]
    own_rows, head_dim = q_all.shape
    q_all[pl.ds(0, early), :] = qa[...]
    q_all[pl.ds(early, late), :] = qb[...]
    for i in range(4):
        for part, rows in (
            (parts[i], pl.ds(i * own_rows, early)),
            (parts[4 + i], pl.ds(i * own_rows + early, late)),
        ):
            k_all[rows, :] = part[:, :head_dim]
            v_all[rows, :] = part[:, head_dim:]
    offsets, wide = EARLY + LATE, 512
    cuts = [slice(start, start + wide) for start in range(0, k_all.shape[0], wide)]

    def one_tile(t, _):
        rows, qpos, qspan = tile_of(t, at_ref, qpos_ref, qspan_ref)
        q = q_all[rows, :]
        peak = jnp.full((TILE, 128), -1e30, jnp.float32)
        for cut in cuts:
            places = []
            for start in range(cut.start, cut.stop, 128):
                o = offsets[start % own_rows // 128]
                origin = start // own_rows
                places.append(kpos_ref[origin : origin + 1, o * 128 : (o + 1) * 128])
            peak = masked_scores(q, k_all[cut, :], places, qpos, qspan, s_all, cut.start, peak)
        top = jnp.broadcast_to(jnp.max(peak, axis=-1, keepdims=True), peak.shape)
        total = jnp.zeros((TILE, 128), jnp.float32)
        mixed = jnp.zeros((TILE, head_dim), jnp.float32)
        for cut in cuts:
            total, mixed = mixing(s_all, cut.start, v_all[cut, :], top, total, mixed)
        result = (mixed / jnp.sum(total, axis=-1, keepdims=True)).astype(jnp.bfloat16)
        for i in range(TILE // 128):
            placed = pl.ds(pl.multiple_of(at_ref[1, t * (TILE // 128) + i] * 128, 128), 128)
            o_ref[placed, :] = result[i * 128 : (i + 1) * 128, :]
        return 0

    lax.fori_loop(0, own_rows // TILE, one_tile, 0)


def attended(at, queries, keyvals, qpos, qspan, kpos):
    rows, head_dim = sum(q.shape[0] for q in queries), queries[0].shape[1]
    keys = sum(k.shape[0] for k in keyvals)
    vmem = pl.BlockSpec(memory_space=pltpu.VMEM)
    return pl.pallas_call(
        attend_kernel,
        in_specs=[pl.BlockSpec(memory_space=pltpu.SMEM)] + [vmem] * 13,
        out_specs=vmem,
        out_shape=jax.ShapeDtypeStruct((rows, head_dim), jnp.bfloat16),
        scratch_shapes=[
            pltpu.VMEM((rows, head_dim), jnp.bfloat16),
            pltpu.VMEM((keys, head_dim), jnp.bfloat16),
            pltpu.VMEM((keys, head_dim), jnp.bfloat16),
            pltpu.VMEM((TILE, keys), jnp.float32),
        ],
        compiler_params=params(24),
        cost_estimate=pl.CostEstimate(
            flops=40 * rows * keys * head_dim, bytes_accessed=4 * keys * head_dim, transcendentals=rows * keys
        ),
    )(at, *queries, *keyvals, qpos, qspan, kpos)


def output_kernel(m_ref, w_ref, x_ref, o_ref, upper_ref, lower_ref):
    mixed = jnp.concatenate([m_ref[h] for h in range(m_ref.shape[0])], axis=1)
    wide = 512
    for t in range(w_ref.shape[1] // wide):
        lanes = slice(t * wide, (t + 1) * wide)
        added = jnp.dot(mixed, w_ref[:, lanes], preferred_element_type=jnp.float32)
        made = (x_ref[:, lanes].astype(jnp.float32) + added).astype(jnp.bfloat16)
        half = made.shape[0] // 2
        o_ref[:, lanes] = made
        upper_ref[:, lanes] = made[:half]
        lower_ref[:, lanes] = made[half:]


def outputs(mixed, w_out, x):
    return pl.pallas_call(
        output_kernel,
        out_shape=[
            jax.ShapeDtypeStruct(x.shape, jnp.bfloat16),
            *[jax.ShapeDtypeStruct((x.shape[0] // 2, x.shape[1]), jnp.bfloat16)] * 2,
        ],
        compiler_params=params(24),
        cost_estimate=pl.CostEstimate(
            flops=2 * 128 * 1024 * 2048, bytes_accessed=6 * MIB, transcendentals=0
        ),
    )(mixed, w_out, x)


def per_device(acts, order, doc_ids, gain, w_query, w_keyval, w_out, head_temp):
    inputs = acts[0]
    width = w_query.shape[2]
    heads = head_temp.shape[1]
    head_dim = width // heads
    yh, z, c = (lax.axis_index(a).astype(jnp.int32) for a in ("yh", "z", "c"))

    upper, lower, by_head = entry(inputs, gain, w_keyval[0], heads)

    blocks = {(0, 0): upper, (0, 1): lower}
    for distance in (1, 2, 3):
        for part in (0, 1):
            blocks[-distance, part] = shifted(blocks[1 - distance, part], "z", 1)
            blocks[distance, part] = shifted(blocks[distance - 1, part], "z", -1)
    blocks[4, 0] = shifted(blocks[-3, 0], "z", 1)
    blocks[4, 1] = shifted(blocks[3, 1], "z", -1)

    def rows_of(offset):
        at_offset = offset if offset <= 4 else offset - ZS
        return [blocks[at_offset, 0], blocks[at_offset, 1]]

    own_w = lax.all_to_all(by_head, "z", 0, 0, tiled=True)
    other_w = shifted(own_w, "yh", 1)
    wkv = assembled(jnp.stack([yh, c]), own_w, shifted(own_w, "c", 1), other_w, shifted(other_w, "c", 1))
    wq = lax.dynamic_slice_in_dim(w_query[0], z * head_dim, head_dim, axis=1)
    temp = lax.dynamic_slice_in_dim(head_temp, z, 1, axis=1)

    grid = order.reshape(2, ZS, 2, -1)
    grid = lax.dynamic_slice_in_dim(jnp.concatenate([grid, grid], axis=1), z, ZS, axis=1)
    grid = jnp.where(yh == 0, grid, grid[::-1])
    grid = jnp.where(c == 0, grid, grid[:, :, ::-1])
    kpos = grid.transpose(0, 2, 1, 3).reshape(4, -1)
    begins = jnp.sum(
        (doc_ids[None, :] < jnp.arange(1, 8, dtype=jnp.int32)[:, None]).astype(jnp.int32), axis=1
    )
    own_pos = kpos[0].reshape(-1, 1)
    began = jnp.max(jnp.where(begins[None, :] <= own_pos, begins[None, :], 0), axis=1, keepdims=True)
    lowest = jnp.int32(-(2**31))
    qspan = own_pos - began + lowest
    qpos = own_pos + lowest

    q_early, kv_early = projected(sum([rows_of(o) for o in EARLY], []), wq, wkv, temp)
    q_late, kv_late = projected(sum([rows_of(o) for o in LATE], []), wq, wkv, temp)
    over_early = shifted(kv_early, "yh", 1)
    _, over_later = lax.optimization_barrier((kv_late, over_early))
    over_late = shifted(kv_late, "yh", 1)
    keyvals = [kv_early, shifted(kv_early, "c", 1), over_early, shifted(over_later, "c", 1)]
    keyvals += [kv_late, shifted(kv_late, "c", 1), over_late, shifted(over_late, "c", 1)]
    offsets = jnp.array(EARLY + LATE, jnp.int32)
    at = jnp.stack([offsets, lax.rem(z + offsets, ZS)])
    mixed = attended(at, [q_early, q_late], keyvals, qpos, qspan, kpos)

    mixed = lax.all_to_all(mixed.reshape(ZS, -1, head_dim), "z", 0, 0, tiled=True)
    produced, *halves = outputs(mixed, w_out[0], inputs)
    handed = jnp.concatenate([passed_along(rows, ("yl", "x"), 1) for rows in halves])
    return (produced[None], handed[None])


def solution(mesh):
    devices = np.asarray(mesh.devices).reshape(2, ZS, 2, 2, 4)
    fine = Mesh(devices, ("yh", "z", "c", "yl", "x"))
    phase, blk = ("yl", "x"), ("yh", "z", "c")
    return jax.shard_map(
        per_device,
        mesh=fine,
        in_specs=(
            P(phase, blk, None),
            P(),
            P(),
            P(phase, None),
            P(phase, None, None),
            P(phase, blk, None),
            P(phase, None, None),
            P(phase, None),
        ),
        out_specs=(P(phase, blk, None), P(phase, blk, None)),
        check_vma=False,
    )
```
